256 devices in a mesh: rep: 4 (over y), exp: 16 (over z, core), tp: 4 (over x).
Axes of the slice: x: 4, y: 4, z: 8, core: 2. Of those that a mesh axis runs over, the one named last changes fastest.
Arguments:
- tokens: bfloat16 [8192, 4096], P(('rep', 'exp'), 'tp'), may hold values from -6 to 6
- expert_id: int32 [8192, 1], P(('rep', 'exp')), may hold values from 0 to 15; in each aligned block of 128 rows (0 to 127, 128 to 255, ...) at most 32 rows name the same one
- route_weight: float32 [8192, 1], P(('rep', 'exp')), may hold values from 0.1 to 0.6
- cluster_id: int32 [128], replicated, may hold values from 0 to 3
- out_grad: bfloat16 [8192, 4096], P(('rep', 'exp'), 'tp'), may hold values from -6 to 6
- w_gate: bfloat16 [16, 4096, 1536], P('exp', None, 'tp'), may hold values from -0.09375 to 0.09375
- w_up: bfloat16 [16, 4096, 1536], P('exp', None, 'tp'), may hold values from -0.09375 to 0.09375
- w_down: bfloat16 [16, 1536, 4096], P('exp', 'tp'), may hold values from -0.15625 to 0.15625
Outputs:
- mixed: bfloat16 [8192, 4096], P(('rep', 'exp'), 'tp')
- grad_tokens: bfloat16 [8192, 4096], P(('rep', 'exp'), 'tp')
- grad_gate: bfloat16 [16, 4096, 1536], P('exp', 'rep', 'tp')
- grad_up: bfloat16 [16, 4096, 1536], P('exp', 'rep', 'tp')
- grad_down: bfloat16 [16, 1536, 4096], P('exp', 'tp', 'rep')
The draws below stay inside these ranges and needn't reach their ends.
Inputs may be any that keep to these rules, and one draw needn't show every extreme that they name: `expert_id`: in each aligned block of 128 tokens (the tokens held by one (rep, exp) position) no expert is named by more than 32 routes, and in every draw some block names some expert exactly 32 times.
All inputs are finite; a program needn't handle non-finite values.
Results may differ from the reference program's by a relative error of at most 0.015.
Values may be sent and summed in bfloat16 or wider, within the bound.
A program may use at most 128 MiB of HBM per device.

```python
import math
import jax
import jax.numpy as jnp
import numpy as np
from jax import lax

D = 4096
FF = 1536
TOK_DEV = 128
TOP = 1
ROLL_DEV = 2
GROUP = 16
VOTES = 4
EXPERTS = 16
C = 32
TOKENS = 8192
ROLLOUTS = 128
N_TP = 4


def place_ends(values, key, smallest, largest):
    longest = values.shape.index(max(values.shape))
    spots = []
    for shift in (0, 1):
        where = [jax.random.randint(jax.random.fold_in(key, axis), (), 0, length) for axis, length in enumerate(values.shape)]
        where[longest] = (where[longest] + shift) % values.shape[longest]
        spots.append(tuple(where))
    return values.at[spots[0]].set(smallest).at[spots[1]].set(largest)


def block_scale(key, shape, split, least, top_value):
    gain = 1.0
    for dim, shards_of in split:
        draws = jax.random.uniform(jax.random.fold_in(jax.random.fold_in(key, 6), dim), (shards_of,), jnp.float32, least / len(split), top_value / len(split))
        gain = gain * jnp.repeat(jnp.exp(draws), shape[dim] // shards_of).reshape((-1,) + (1,) * (len(shape) - 1 - dim))
    return gain


def routed_block(rng, own, number, rows, amount, top, limit, lean):
    sequence = jax.random.permutation(rng, amount)
    crowded, usual = portions_of(amount, rows * top, limit, lean, True), portions_of(amount, rows * top, limit, lean, False)
    places = jnp.arange(amount)

    def named(tallies, rotation):
        used = int((tallies > 0).sum())
        fixed = max(1, used // 4)
        passed = fixed + (places - fixed + rotation * (used - fixed)) % max(1, amount - fixed)
        return jnp.zeros((amount,), jnp.int32).at[sequence[jnp.where(places < fixed, places, passed)]].set(jnp.asarray(tallies, jnp.int32))

    tallies = jnp.where(number % 4 == 0, named(crowded, number // 4), named(usual, number - number // 4 - 1))
    mixed = jax.random.permutation(jax.random.fold_in(own, 3), amount)
    donor, sink = mixed[0:amount // 2 * 2:2], mixed[1:amount // 2 * 2:2]
    margin = jnp.minimum(tallies[donor] - 1, limit - tallies[sink]) // 2
    margin = jnp.where((donor == sequence[0]) | (sink == sequence[0]) | (tallies[sink] == 0), 0, jnp.maximum(margin, 0))
    passed = jax.random.randint(jax.random.fold_in(own, 4), (amount // 2,), 0, 1 << 20) % (margin + 1)
    tallies = tallies.at[donor].add(-passed).at[sink].add(passed)
    members = jnp.searchsorted(jnp.cumsum(tallies), jnp.arange(rows * top), side="right").astype(jnp.int32)
    listing = members.reshape(top, rows).T
    listing = listing[jax.random.permutation(jax.random.fold_in(own, 1), rows)]
    rotation = jax.random.randint(jax.random.fold_in(own, 2), (rows, 1), 0, top)
    return jnp.take_along_axis(listing, (jnp.arange(top)[None, :] + rotation) % top, axis=1)


def portions_of(number_of, total, limit, skew, full):
    portions = [(1 << 20) // math.isqrt(grade ** skew) + 1 for grade in range(1, number_of + 1)]
    largest = limit if full else min(limit, max(-(-total // number_of), total * portions[0] // sum(portions)))
    least = 1 if total - largest >= number_of - 1 else 0
    given, surplus = [largest] + [least] * (number_of - 1), total - largest - least * (number_of - 1)
    while surplus > 0:
        candidates = [i for i in range(1, number_of) if given[i] < largest] or [i for i in range(1, number_of) if given[i] < limit]
        pool, remaining = sum([portions[i] for i in candidates]), surplus
        for i in candidates:
            more = min(limit - given[i], max(1, remaining * portions[i] // pool), surplus)
            given[i] = given[i] + more
            surplus = surplus - more
    return np.array(given)


def scatter_about(rng, dims, spread, reach, cuts=(), kind=jnp.bfloat16):
    factor_of = block_scale(rng, dims, cuts, -0.22, 0.18) if cuts else 1.0
    array = jax.random.normal(rng, dims, jnp.float32) * spread * factor_of
    return jnp.minimum(jnp.maximum(array, -reach), reach).astype(kind)


def setup_inputs(seed: int = 0) -> dict:
    arg_keys = jax.random.split(jax.random.key(seed), 9)
    tokens = scatter_about(arg_keys[0], (TOKENS, D), 1.0, 6.0, ((0, 64), (1, 4)))
    expert_id_keys = jax.random.split(jax.random.fold_in(arg_keys[1], 1), TOKENS // TOK_DEV)
    expert_id_turns = jax.random.permutation(jax.random.fold_in(arg_keys[1], 3), TOKENS // TOK_DEV)
    expert_id = jax.vmap(lambda own, number: routed_block(jax.random.fold_in(arg_keys[1], 2), own, number, TOK_DEV, EXPERTS, TOP, C, 2))(expert_id_keys, expert_id_turns).reshape((TOKENS, TOP))
    route_weight = jnp.clip(0.1 + 0.5 * jax.random.uniform(arg_keys[2], (TOKENS, TOP), jnp.float32) ** block_scale(arg_keys[2], (TOKENS, TOP), ((0, 64),), -0.2, 0.2), 0.1, 0.6)
    cluster_id = place_ends(jax.random.randint(arg_keys[3], (ROLLOUTS,), 0, VOTES), jax.random.fold_in(arg_keys[3], 1), 0, VOTES - 1).astype(jnp.int32)
    out_grad = scatter_about(arg_keys[4], (TOKENS, D), 1.0, 6.0, ((0, 64), (1, 4)))
    w_gate = scatter_about(arg_keys[5], (EXPERTS, D, FF), D ** -0.5, 0.09375, ((0, 16), (2, 4)))
    w_up = scatter_about(arg_keys[6], (EXPERTS, D, FF), D ** -0.5, 0.09375, ((0, 16), (2, 4)))
    w_down = scatter_about(arg_keys[7], (EXPERTS, FF, D), FF ** -0.5, 0.15625, ((0, 16), (1, 4)))
    return {"tokens": tokens, "expert_id": expert_id, "route_weight": route_weight, "cluster_id": cluster_id, "out_grad": out_grad, "w_gate": w_gate, "w_up": w_up, "w_down": w_down}


def vote_advantage(cluster_id):
    total_rollouts = cluster_id.shape[0]
    group_of = jnp.arange(total_rollouts, dtype=jnp.int32) // GROUP
    same_vote = (cluster_id[:, None] == cluster_id[None, :]) & (group_of[:, None] == group_of[None, :])
    agreement = jnp.sum(same_vote.astype(jnp.float32), axis=1)
    group_mean = jnp.mean(agreement.reshape(total_rollouts // GROUP, GROUP), axis=1)
    return agreement - jnp.repeat(group_mean, GROUP)


def split_products(left_mat, right_mat):
    row_count = left_mat.shape[0]
    piece_width = left_mat.shape[1] // N_TP
    left_split = left_mat.reshape(row_count, N_TP, piece_width).astype(jnp.float32)
    right_split = right_mat.reshape(N_TP, piece_width, right_mat.shape[1]).astype(jnp.float32)
    return jnp.einsum('rkf,kfd->krd', left_split, right_split, precision=lax.Precision.HIGHEST)


def round_pieces(pieces):
    rounded = lax.optimization_barrier(pieces.astype(jnp.bfloat16))
    return jnp.sum(rounded.astype(jnp.float32), axis=0).astype(jnp.bfloat16)


def reference(tokens, expert_id, route_weight, cluster_id, out_grad, w_gate, w_up, w_down):
    token_count = tokens.shape[0]
    advantage = vote_advantage(cluster_id)
    token_advantage = jnp.repeat(advantage, TOK_DEV // ROLL_DEV)
    weight = route_weight[:, 0]
    cotangent = ((token_advantage * weight)[:, None] * out_grad.astype(jnp.float32)).astype(jnp.bfloat16)
    expert_ids = expert_id[:, 0].astype(jnp.int32)
    sorted_order = jnp.argsort(expert_ids, stable=True).astype(jnp.int32)
    onehot = (expert_ids[:, None] == jnp.arange(EXPERTS, dtype=jnp.int32)[None, :]).astype(jnp.int32)
    counts = jnp.sum(onehot, axis=0).astype(jnp.int32)
    padded = ((counts + 127) // 128 * 128).astype(jnp.int32)
    starts = (jnp.cumsum(padded) - padded).astype(jnp.int32)
    firsts = (jnp.cumsum(counts) - counts).astype(jnp.int32)
    sorted_ids = expert_ids[sorted_order]
    slot_of = (starts[sorted_ids] + jnp.arange(token_count, dtype=jnp.int32) - firsts[sorted_ids]).astype(jnp.int32)
    block_total = token_count // 128 + EXPERTS
    source = jnp.full((block_total * 128,), token_count, jnp.int32).at[slot_of].set(sorted_order)
    block_ends = starts + padded
    positions = jnp.arange(block_total, dtype=jnp.int32) * 128
    block_expert = jnp.minimum(jnp.sum((block_ends[None, :] <= positions[:, None]).astype(jnp.int32), axis=1), EXPERTS - 1).astype(jnp.int32)
    token_slot = jnp.zeros((token_count,), jnp.int32).at[sorted_order].set(slot_of)
    zero_row = jnp.zeros((1, D), jnp.bfloat16)
    token_pad = jnp.concatenate([tokens, zero_row], axis=0)
    cot_pad = jnp.concatenate([cotangent, zero_row], axis=0)
    zero_grads = (jnp.zeros((EXPERTS, D, FF), jnp.float32), jnp.zeros((EXPERTS, D, FF), jnp.float32), jnp.zeros((EXPERTS, FF, D), jnp.float32))

    def block_step(carry, index):
        grad_g, grad_u, grad_d = carry
        expert = block_expert[index]
        row_index = lax.dynamic_slice_in_dim(source, (index * 128).astype(jnp.int32), 128)
        block_x = token_pad[row_index]
        block_cot = cot_pad[row_index]
        gate_mat = w_gate[expert]
        up_mat = w_up[expert]
        down_mat = w_down[expert]
        pre_gate = jnp.dot(block_x, gate_mat, preferred_element_type=jnp.float32)
        pre_up = jnp.dot(block_x, up_mat, preferred_element_type=jnp.float32)
        sigmoid_gate = jax.nn.sigmoid(pre_gate)
        silu_gate = pre_gate * sigmoid_gate
        hidden = (silu_gate * pre_up).astype(jnp.bfloat16)
        out_block = round_pieces(split_products(hidden, down_mat))
        grad_hidden = jnp.dot(block_cot, down_mat.T, preferred_element_type=jnp.float32)
        grad_pre_gate = (grad_hidden * pre_up * sigmoid_gate * (1.0 + pre_gate * (1.0 - sigmoid_gate))).astype(jnp.bfloat16)
        grad_pre_up = (grad_hidden * silu_gate).astype(jnp.bfloat16)
        in_block = round_pieces(split_products(grad_pre_gate, gate_mat.T) + split_products(grad_pre_up, up_mat.T))
        grad_g = grad_g.at[expert].add(jnp.dot(block_x.T, grad_pre_gate, preferred_element_type=jnp.float32))
        grad_u = grad_u.at[expert].add(jnp.dot(block_x.T, grad_pre_up, preferred_element_type=jnp.float32))
        grad_d = grad_d.at[expert].add(jnp.dot(hidden.T, block_cot, preferred_element_type=jnp.float32))
        return (grad_g, grad_u, grad_d), (out_block, in_block)

    carry, (out_blocks, in_blocks) = lax.scan(block_step, zero_grads, jnp.arange(block_total, dtype=jnp.int32))
    out_rows = out_blocks.reshape(block_total * 128, D)
    in_rows = in_blocks.reshape(block_total * 128, D)
    mixed = (weight[:, None] * out_rows[token_slot].astype(jnp.float32)).astype(jnp.bfloat16)
    grad_tokens = in_rows[token_slot]
    return (mixed, grad_tokens, carry[0].astype(jnp.bfloat16), carry[1].astype(jnp.bfloat16), carry[2].astype(jnp.bfloat16))
```

```python
import jax
import jax.numpy as jnp
from jax import lax
from jax.experimental import pallas as pl
from jax.experimental.pallas import tpu as pltpu
from jax.sharding import PartitionSpec as P

MESH = pl.DeviceIdType.MESH
F32, BF16 = jnp.float32, jnp.bfloat16
TOK = 128
CAP = 32
NE = 16
ROWS = NE * CAP
FB = 1024
HID = 384
GROUP = 16
CH = 4
CROWS = ROWS // CH
HALVES = 2
HROWS = ROWS // HALVES
QROWS = HROWS // 2
FAR = (0, 1, 7, 2, 6, 3, 5, 4)


def dot_nn(a, b):
    return lax.dot_general(a, b, (((1,), (0,)), ((), ())), preferred_element_type=F32)


def dot_nt(a, b):
    return lax.dot_general(a, b, (((1,), (1,)), ((), ())), preferred_element_type=F32)


def dot_tn(a, b):
    return lax.dot_general(a, b, (((0,), (0,)), ((), ())), preferred_element_type=F32)


def kernel(
    tokens,
    eid_col,
    eid_row,
    weight,
    clu_col,
    clu_row,
    out_grad,
    w_gate,
    w_up,
    w_down,
    mixed,
    grad_tokens,
    out_gate,
    out_up,
    out_down,
    send_t,
    send_c,
    rows_t,
    rows_c,
    wg,
    wu,
    wd,
    slope,
    silu,
    hidden,
    gpre,
    part_o,
    x_one,
    x_left,
    x_right,
    ret,
    g_gu,
    g_dn,
    y_one_gu,
    y_one_dn,
    y_left_gu,
    y_left_dn,
    y_right_gu,
    y_right_dn,
    w_sem,
    z_ssem,
    z_rsem,
    ag_ssem,
    ag_rsem,
    rs_ssem,
    rs_rsem,
    zr_ssem,
    zr_rsem,
    y_ssem,
    y_rsem,
):
    x, y, e = lax.axis_index("tp"), lax.axis_index("rep"), lax.axis_index("exp")
    z, core = e // 2, e % 2
    x_next, x_prev = {"tp": (x + 1) % 4}, {"tp": (x + 3) % 4}
    y_next, y_prev = {"rep": (y + 1) % 4}, {"rep": (y + 3) % 4}

    def to_of(j):
        return {"exp": ((z + FAR[j // 2]) % 8) * 2 + (core + j % 2) % 2}

    def from_of(j):
        return {"exp": ((z + 8 - FAR[j // 2]) % 8) * 2 + (core + j % 2) % 2}

    sends = []

    def remote(src, dst, ssem, rsem, where):
        return pltpu.make_async_remote_copy(
            src_ref=src,
            dst_ref=dst,
            send_sem=ssem,
            recv_sem=rsem,
            device_id=where,
            device_id_type=MESH,
        )

    loads = []
    for i in range(4):
        at = pl.ds(pl.multiple_of(((x + i) % 4) * FB, FB), FB)
        loads.append(pltpu.make_async_copy(w_gate.at[0, at, :], wg.at[i], w_sem.at[i]))
        loads.append(pltpu.make_async_copy(w_up.at[0, at, :], wu.at[i], w_sem.at[4 + i]))
        loads.append(pltpu.make_async_copy(w_down.at[0, :, at], wd.at[i], w_sem.at[8 + i]))
    for load in loads:
        load.start()

    barrier = pltpu.get_barrier_semaphore()
    for where in [to_of(j) for j in range(1, NE)] + [x_next, x_prev, y_next, y_prev]:
        pl.semaphore_signal(barrier, inc=1, device_id=where, device_id_type=MESH)

    def place(ids):
        away = ((ids >> 1) - z + 8) & 7
        first = jnp.where(away == 0, 0, jnp.where(away <= 4, 2 * away - 1, 16 - 2 * away))
        return (2 * first + (((ids & 1) + core) & 1)) * CAP

    ids_col, ids_row = eid_col[...], eid_row[...]
    sub = lax.broadcasted_iota(jnp.int32, (TOK, TOK), 0)
    lane = lax.broadcasted_iota(jnp.int32, (TOK, TOK), 1)
    same = ids_col == ids_row
    rank_col = jnp.sum(jnp.where(same & (lane < sub), 1.0, 0.0), axis=1, keepdims=True)
    rank_row = jnp.sum(jnp.where(same & (sub < lane), 1.0, 0.0), axis=0, keepdims=True)
    slot_col = place(ids_col) + rank_col.astype(jnp.int32)
    slot_row = place(ids_row) + rank_row.astype(jnp.int32)
    pick = jnp.where(
        lax.broadcasted_iota(jnp.int32, (ROWS, TOK), 0) == slot_row, 1.0, 0.0
    ).astype(BF16)
    send_t[...] = dot_nn(pick, tokens[...]).astype(BF16)

    pl.semaphore_wait(barrier, NE - 1 + 4)

    def z_copy(k, j):
        src, dst = ((send_t, rows_t), (send_c, rows_c))[k]
        at = pl.ds(j * CAP, CAP)
        return remote(src.at[at], dst.at[0, at], z_ssem.at[k, j], z_rsem.at[k, j], to_of(j))

    for j in range(1, NE):
        z_copy(0, j).start()
    rows_t[0, 0:CAP, :] = send_t[0:CAP, :]

    same_group = (sub // GROUP) == (lane // GROUP)
    votes = jnp.where((clu_col[...] == clu_row[...]) & same_group, 1.0, 0.0)
    agree_row = jnp.sum(votes, axis=0, keepdims=True)
    agree_col = jnp.sum(votes, axis=1, keepdims=True)
    mean_row = jnp.sum(jnp.where(same_group, agree_col, 0.0), axis=0, keepdims=True) * (1.0 / GROUP)
    own = 2 * (y * NE + e) + sub // (TOK // 2)
    adv = jnp.sum(jnp.where(lane == own, agree_row - mean_row, 0.0), axis=1, keepdims=True)
    cot = ((adv * weight[...]) * out_grad[...].astype(F32)).astype(BF16)
    send_c[...] = dot_nn(pick, cot).astype(BF16)
    for j in range(1, NE):
        z_copy(1, j).start()
    rows_c[0, 0:CAP, :] = send_c[0:CAP, :]

    def ag_copies(k, c):
        buf = (rows_t, rows_c)[k]
        lo = pl.ds(c * CROWS, CROWS)
        a = pl.ds(c * CROWS, CROWS // 2)
        b = pl.ds(c * CROWS + CROWS // 2, CROWS // 2)
        s, r = ag_ssem, ag_rsem
        return (
            remote(buf.at[0, lo], buf.at[3, lo], s.at[k, c, 0], r.at[k, c, 0], x_next),
            remote(buf.at[0, lo], buf.at[1, lo], s.at[k, c, 1], r.at[k, c, 1], x_prev),
            remote(buf.at[3, a], buf.at[2, a], s.at[k, c, 2], r.at[k, c, 2], x_next),
            remote(buf.at[1, b], buf.at[2, b], s.at[k, c, 3], r.at[k, c, 3], x_prev),
        )

    def ag_send(k, c):
        for j in range(max(4 * c, 1), 4 * c + 4):
            z_copy(k, j).wait_recv()
        for copy in ag_copies(k, c)[:2]:
            copy.start()

    def ag_forward(k, c):
        copies = ag_copies(k, c)
        copies[0].wait_recv()
        copies[2].start()
        copies[1].wait_recv()
        copies[3].start()

    def ag_wait(k, c):
        for copy in ag_copies(k, c)[2:]:
            copy.wait_recv()

    def hrows(m):
        return pl.ds(m * HROWS, HROWS)

    def first_layer(m):
        at = hrows(m)
        pre_g = dot_nn(rows_t[0, at, :], wg[0])
        for i in range(1, 4):
            pre_g += dot_nn(rows_t[i, at, :], wg[i])
        slope[at, :] = pre_g
        pre_u = dot_nn(rows_t[0, at, :], wu[0])
        for i in range(1, 4):
            pre_u += dot_nn(rows_t[i, at, :], wu[i])
        pre_g = slope[at, :]
        sig = jax.nn.sigmoid(pre_g)
        act = pre_g * sig
        hidden[at, :] = (act * pre_u).astype(BF16)
        silu[at, :] = act
        slope[at, :] = pre_u * sig * (1.0 + pre_g * (1.0 - sig))

    def second_layer(m):
        @pl.loop(0, 4)
        def _(i):
            part_o[i, hrows(m), :] = dot_nn(hidden[hrows(m), :], wd[i]).astype(BF16)

    def back_hidden(m):
        at = hrows(m)
        grad = dot_nt(rows_c[0, at, :], wd[0])
        for i in range(1, 4):
            grad += dot_nt(rows_c[i, at, :], wd[i])
        gpre[at, 0:HID] = (grad * slope[at, :]).astype(BF16)
        gpre[at, HID:] = (grad * silu[at, :]).astype(BF16)

    part_i = rows_t

    def back_tokens(m):
        @pl.loop(0, 4)
        def _(i):
            part_i[i, hrows(m), :] = (
                dot_nt(gpre[hrows(m), 0:HID], wg[i]) + dot_nt(gpre[hrows(m), HID:], wu[i])
            ).astype(BF16)

    ORDER = (2, 1, 3, 0)

    def weight_grads(k):
        i = (y + ORDER[k] - x + 4) % 4

        @pl.loop(0, 4)
        def _(f):
            at = pl.ds(pl.multiple_of(f * 256, 256), 256)
            g_gu[k, at, :] = dot_tn(rows_t[i, :, at], gpre[...]).astype(BF16)
            g_dn[k, :, at] = dot_tn(hidden[...], rows_c[i, :, at]).astype(BF16)

    def rs_copies(k, m):
        part = (part_o, part_i)[k]
        a, b = pl.ds(m * HROWS, QROWS), pl.ds(m * HROWS + QROWS, QROWS)
        s, r = rs_ssem, rs_rsem
        return (
            remote(part.at[2, a], x_one.at[k, m, 0], s.at[k, m, 0], r.at[k, m, 0], x_next),
            remote(part.at[2, b], x_one.at[k, m, 1], s.at[k, m, 1], r.at[k, m, 1], x_prev),
            remote(part.at[1, b], x_left.at[k, b], s.at[k, m, 2], r.at[k, m, 2], x_next),
            remote(part.at[3, a], x_right.at[k, a], s.at[k, m, 3], r.at[k, m, 3], x_prev),
            remote(part.at[1, a], x_left.at[k, a], s.at[k, m, 4], r.at[k, m, 4], x_next),
            remote(part.at[3, b], x_right.at[k, b], s.at[k, m, 5], r.at[k, m, 5], x_prev),
        )

    def add_into(ref, at, other):
        ref[at] = (ref[at].astype(F32) + other.astype(F32)).astype(BF16)

    def rs_first(k):
        for m in range(HALVES):
            for copy in rs_copies(k, m)[:2]:
                copy.start()
        for m in range(HALVES):
            for copy in rs_copies(k, m)[2:4]:
                copy.start()

    def rs_pass_on(k, m):
        part = (part_o, part_i)[k]
        copies = rs_copies(k, m)
        copies[0].wait_recv()
        add_into(part, (1, pl.ds(m * HROWS, QROWS)), x_one[k, m, 0])
        copies[4].start()
        copies[1].wait_recv()
        add_into(part, (3, pl.ds(m * HROWS + QROWS, QROWS)), x_one[k, m, 1])
        copies[5].start()

    total = (send_t, send_c)

    def zr_copy(k, j):
        at = pl.ds(j * CAP, CAP)
        return remote(
            total[k].at[at], ret.at[k, at], zr_ssem.at[k, j], zr_rsem.at[k, j], from_of(j)
        )

    def rs_last(k, m):
        part = (part_o, part_i)[k]
        for copy in rs_copies(k, m)[2:]:
            copy.wait_recv()
        at = hrows(m)
        total[k][at, :] = (
            part[0, at, :].astype(F32)
            + x_left[k, at, :].astype(F32)
            + x_right[k, at, :].astype(F32)
        ).astype(BF16)
        for j in reversed(range(max(m * 8, 1), m * 8 + 8)):
            zr_copy(k, j).start()
        if m == 0:
            ret[k, 0:CAP, :] = total[k][0:CAP, :]

    def back(k):
        for j in range(1, NE):
            zr_copy(k, j).wait_recv()
        spread = jnp.where(
            lax.broadcasted_iota(jnp.int32, (TOK, ROWS), 1) == slot_col, 1.0, 0.0
        ).astype(BF16)
        return dot_nn(spread, ret[k])

    def y_copies():
        s, r = y_ssem, y_rsem
        gu_a, gu_b = pl.ds(0, FB // 2), pl.ds(FB // 2, FB // 2)
        dn_a, dn_b = pl.ds(0, HID // 2), pl.ds(HID // 2, HID // 2)
        return (
            (
                remote(g_gu.at[0, gu_a], y_one_gu.at[0], s.at[0], r.at[0], y_next),
                remote(g_dn.at[0, dn_a], y_one_dn.at[0], s.at[1], r.at[1], y_next),
                remote(g_gu.at[0, gu_b], y_one_gu.at[1], s.at[2], r.at[2], y_prev),
                remote(g_dn.at[0, dn_b], y_one_dn.at[1], s.at[3], r.at[3], y_prev),
            ),
            (
                remote(g_gu.at[1, gu_b], y_left_gu.at[gu_b], s.at[4], r.at[4], y_next),
                remote(g_dn.at[1, dn_b], y_left_dn.at[dn_b], s.at[5], r.at[5], y_next),
            ),
            (
                remote(g_gu.at[2, gu_a], y_right_gu.at[gu_a], s.at[6], r.at[6], y_prev),
                remote(g_dn.at[2, dn_a], y_right_dn.at[dn_a], s.at[7], r.at[7], y_prev),
            ),
            (
                remote(g_gu.at[1, gu_a], y_left_gu.at[gu_a], s.at[8], r.at[8], y_next),
                remote(g_dn.at[1, dn_a], y_left_dn.at[dn_a], s.at[9], r.at[9], y_next),
                remote(g_gu.at[2, gu_b], y_right_gu.at[gu_b], s.at[10], r.at[10], y_prev),
                remote(g_dn.at[2, dn_b], y_right_dn.at[dn_b], s.at[11], r.at[11], y_prev),
            ),
        )

    ag_send(0, 0)
    ag_send(0, 1)
    ag_forward(0, 0)
    ag_send(0, 2)
    ag_forward(0, 1)
    ag_send(0, 3)
    ag_forward(0, 2)
    ag_send(1, 0)
    ag_forward(0, 3)
    ag_send(1, 1)
    for load in loads:
        load.wait()
    ag_wait(0, 0)
    ag_wait(0, 1)
    first_layer(0)
    ag_send(1, 2)
    ag_forward(1, 0)
    ag_send(1, 3)
    ag_wait(0, 2)
    ag_wait(0, 3)
    first_layer(1)
    ag_forward(1, 1)
    second_layer(0)
    second_layer(1)
    ag_forward(1, 2)
    ag_wait(1, 0)
    ag_wait(1, 1)
    back_hidden(0)
    ag_forward(1, 3)
    rs_first(0)
    ag_wait(1, 2)
    ag_wait(1, 3)
    back_hidden(1)
    ys = y_copies()
    weight_grads(0)
    for copy in ys[0]:
        copy.start()
    weight_grads(1)
    for copy in ys[1]:
        copy.start()
    weight_grads(2)
    for copy in ys[2]:
        copy.start()
    rs_pass_on(0, 0)
    rs_pass_on(0, 1)
    weight_grads(3)
    for c in range(CH):
        for copy in ag_copies(0, c):
            copy.wait_send()
    back_tokens(0)
    back_tokens(1)
    rs_first(1)
    for k in range(2):
        for j in range(1, NE):
            z_copy(k, j).wait_send()
    rs_last(0, 0)
    for copy in ys[0]:
        copy.wait_recv()
    FH, HH = FB // 2, HID // 2
    add_into(g_gu, (1, pl.ds(0, FH)), y_one_gu[0])
    add_into(g_dn, (1, pl.ds(0, HH)), y_one_dn[0])
    ys[3][0].start()
    ys[3][1].start()
    add_into(g_gu, (2, pl.ds(FH, FH)), y_one_gu[1])
    add_into(g_dn, (2, pl.ds(HH, HH)), y_one_dn[1])
    ys[3][2].start()
    ys[3][3].start()
    rs_last(0, 1)
    rs_pass_on(1, 0)
    rs_pass_on(1, 1)
    rs_last(1, 0)
    rs_last(1, 1)
    mixed[...] = (weight[...] * back(0).astype(BF16).astype(F32)).astype(BF16)
    for copy in ys[1] + ys[2] + ys[3]:
        copy.wait_recv()
    both = (
        g_gu[3].astype(F32) + y_left_gu[...].astype(F32) + y_right_gu[...].astype(F32)
    ).astype(BF16)
    out_gate[0] = both[:, :HID]
    out_up[0] = both[:, HID:]
    out_down[0] = (
        g_dn[3].astype(F32) + y_left_dn[...].astype(F32) + y_right_dn[...].astype(F32)
    ).astype(BF16)
    grad_tokens[...] = back(1).astype(BF16)

    for c in range(CH):
        for copy in ag_copies(1, c):
            copy.wait_send()
    for k in range(2):
        for m in range(HALVES):
            for copy in rs_copies(k, m):
                copy.wait_send()
        for j in range(1, NE):
            zr_copy(k, j).wait_send()
    for group in ys:
        for copy in group:
            copy.wait_send()


def body(tokens, expert_id, route_weight, cluster_id, out_grad, w_gate, w_up, w_down):
    vmem, far = pl.BlockSpec(memory_space=pltpu.VMEM), pl.BlockSpec(memory_space=pl.ANY)
    dma = pltpu.SemaphoreType.DMA
    rollouts = cluster_id.shape[0]
    return pl.pallas_call(
        kernel,
        out_shape=(
            jax.ShapeDtypeStruct((TOK, FB), BF16),
            jax.ShapeDtypeStruct((TOK, FB), BF16),
            jax.ShapeDtypeStruct((1, FB, HID), BF16),
            jax.ShapeDtypeStruct((1, FB, HID), BF16),
            jax.ShapeDtypeStruct((1, HID, FB), BF16),
        ),
        in_specs=[vmem] * 7 + [far] * 3,
        out_specs=(vmem,) * 5,
        scratch_shapes=[
            pltpu.VMEM((ROWS, FB), BF16),
            pltpu.VMEM((ROWS, FB), BF16),
            pltpu.VMEM((4, ROWS, FB), BF16),
            pltpu.VMEM((4, ROWS, FB), BF16),
            pltpu.VMEM((4, FB, HID), BF16),
            pltpu.VMEM((4, FB, HID), BF16),
            pltpu.VMEM((4, HID, FB), BF16),
            pltpu.VMEM((ROWS, HID), F32),
            pltpu.VMEM((ROWS, HID), F32),
            pltpu.VMEM((ROWS, HID), BF16),
            pltpu.VMEM((ROWS, 2 * HID), BF16),
            pltpu.VMEM((4, ROWS, FB), BF16),
            pltpu.VMEM((2, HALVES, 2, QROWS, FB), BF16),
            pltpu.VMEM((2, ROWS, FB), BF16),
            pltpu.VMEM((2, ROWS, FB), BF16),
            pltpu.VMEM((2, ROWS, FB), BF16),
            pltpu.VMEM((4, FB, 2 * HID), BF16),
            pltpu.VMEM((4, HID, FB), BF16),
            pltpu.VMEM((2, FB // 2, 2 * HID), BF16),
            pltpu.VMEM((2, HID // 2, FB), BF16),
            pltpu.VMEM((FB, 2 * HID), BF16),
            pltpu.VMEM((HID, FB), BF16),
            pltpu.VMEM((FB, 2 * HID), BF16),
            pltpu.VMEM((HID, FB), BF16),
            dma((12,)),
            dma((2, NE)),
            dma((2, NE)),
            dma((2, CH, 4)),
            dma((2, CH, 4)),
            dma((2, HALVES, 6)),
            dma((2, HALVES, 6)),
            dma((2, NE)),
            dma((2, NE)),
            dma((12,)),
            dma((12,)),
        ],
        compiler_params=pltpu.CompilerParams(
            collective_id=0, has_side_effects=True, vmem_limit_bytes=60 * 2**20
        ),
        name="expert_layer",
    )(
        tokens,
        expert_id,
        expert_id.reshape(1, TOK),
        route_weight,
        cluster_id.reshape(rollouts, 1),
        cluster_id.reshape(1, rollouts),
        out_grad,
        w_gate,
        w_up,
        w_down,
    )


def solution(mesh):
    placed = (
        P(("rep", "exp"), "tp"),
        P(("rep", "exp"), None),
        P(("rep", "exp"), None),
        P(),
        P(("rep", "exp"), "tp"),
        P("exp", None, "tp"),
        P("exp", None, "tp"),
        P("exp", "tp", None),
    )
    return jax.shard_map(
        body,
        mesh=mesh,
        in_specs=placed,
        out_specs=(
            P(("rep", "exp"), "tp"),
            P(("rep", "exp"), "tp"),
            P("exp", "rep", "tp"),
            P("exp", "rep", "tp"),
            P("exp", "tp", "rep"),
        ),
        check_vma=False,
    )
```

```python
import jax
import jax.numpy as jnp
from jax import lax
from jax.experimental import pallas as pl
from jax.experimental.pallas import tpu as pltpu
from jax.sharding import PartitionSpec as P

MESH = pl.DeviceIdType.MESH
F32, BF16 = jnp.float32, jnp.bfloat16
TOK = 128
CAP = 32
NE = 16
ROWS = NE * CAP
FB = 1024
HID = 384
GROUP = 16
LIMIT = 56
CH = 4
CROWS = ROWS // CH
HROWS = ROWS // 2
QROWS = CROWS // 2
FAR = (0, 1, 7, 2, 6, 3, 5, 4)


def dot_nn(a, b):
    return lax.dot_general(a, b, (((1,), (0,)), ((), ())), preferred_element_type=F32)


def dot_nt(a, b):
    return lax.dot_general(a, b, (((1,), (1,)), ((), ())), preferred_element_type=F32)


def dot_tn(a, b):
    return lax.dot_general(a, b, (((0,), (0,)), ((), ())), preferred_element_type=F32)


def kernel(
    eid_row,
    weight_row,
    clu_row,
    tokens_far,
    out_grad_far,
    w_gate,
    w_up,
    w_down,
    mixed,
    grad_tokens,
    out_gate,
    out_up,
    out_down,
    tokens,
    out_grad,
    send_t,
    send_c,
    rows_t,
    rows_c,
    wg,
    wu,
    wd,
    slope,
    silu,
    hidden,
    gpre,
    part_o,
    x_one,
    x_left,
    x_right,
    ret,
    g_gu,
    g_dn,
    y_one_gu,
    y_one_dn,
    y_left_gu,
    y_left_dn,
    y_right_gu,
    y_right_dn,
    w_sem,
    z_ssem,
    z_rsem,
    ag_ssem,
    ag_rsem,
    rs_ssem,
    rs_rsem,
    zr_ssem,
    zr_rsem,
    y_ssem,
    y_rsem,
):
    x, y, e = lax.axis_index("tp"), lax.axis_index("rep"), lax.axis_index("exp")
    z, core = e // 2, e % 2
    x_next, x_prev = {"tp": (x + 1) % 4}, {"tp": (x + 3) % 4}
    y_next, y_prev = {"rep": (y + 1) % 4}, {"rep": (y + 3) % 4}

    def to_of(j):
        return {"exp": ((z + FAR[j // 2]) % 8) * 2 + (core + j % 2) % 2}

    def from_of(j):
        return {"exp": ((z + 8 - FAR[j // 2]) % 8) * 2 + (core + j % 2) % 2}

    sends = []

    def remote(src, dst, ssem, rsem, where):
        return pltpu.make_async_remote_copy(
            src_ref=src,
            dst_ref=dst,
            send_sem=ssem,
            recv_sem=rsem,
            device_id=where,
            device_id_type=MESH,
        )

    barrier = pltpu.get_barrier_semaphore()
    for where in [to_of(j) for j in range(1, NE)] + [x_next, x_prev, y_next, y_prev]:
        pl.semaphore_signal(barrier, inc=1, device_id=where, device_id_type=MESH)
    load_t = pltpu.make_async_copy(tokens_far, tokens, w_sem.at[12])
    load_t.start()
    load_c = pltpu.make_async_copy(out_grad_far, out_grad, w_sem.at[13])
    load_c.start()

    loads = []
    for i in range(4):
        at = pl.ds(pl.multiple_of(((x + i) % 4) * FB, FB), FB)
        loads.append(pltpu.make_async_copy(w_gate.at[0, at, :], wg.at[i], w_sem.at[i]))
        loads.append(pltpu.make_async_copy(w_up.at[0, at, :], wu.at[i], w_sem.at[4 + i]))
        loads.append(pltpu.make_async_copy(w_down.at[0, :, at], wd.at[i], w_sem.at[8 + i]))
    for load in loads:
        load.start()

    def place(ids):
        away = ((ids >> 1) - z + 8) & 7
        first = jnp.where(away == 0, 0, jnp.where(away <= 4, 2 * away - 1, 16 - 2 * away))
        return (2 * first + (((ids & 1) + core) & 1)) * CAP

    sub = lax.broadcasted_iota(jnp.int32, (TOK, TOK), 0)
    lane = lax.broadcasted_iota(jnp.int32, (TOK, TOK), 1)

    def column(row):
        return jnp.sum(jnp.where(sub == lane, row, 0), axis=1, keepdims=True)

    ids_row = eid_row[...]
    ids_col = column(ids_row)
    same = ids_col == ids_row
    rank_col = jnp.sum(jnp.where(same & (lane < sub), 1.0, 0.0), axis=1, keepdims=True)
    rank_row = jnp.sum(jnp.where(same & (sub < lane), 1.0, 0.0), axis=0, keepdims=True)
    slot_col = place(ids_col) + rank_col.astype(jnp.int32)
    slot_row = place(ids_row) + rank_row.astype(jnp.int32)
    pick = jnp.where(
        lax.broadcasted_iota(jnp.int32, (ROWS, TOK), 0) == slot_row, 1.0, 0.0
    ).astype(BF16)
    load_t.wait()
    send_t[...] = dot_nn(pick, tokens[...]).astype(BF16)

    pl.semaphore_wait(barrier, NE - 1 + 4)

    def z_copy(k, j):
        src, dst = ((send_t, rows_t), (send_c, rows_c))[k]
        at = pl.ds(j * CAP, CAP)
        return remote(src.at[at], dst.at[0, at], z_ssem.at[k, j], z_rsem.at[k, j], to_of(j))

    def z_start(k, c):
        for j in range(max(4 * c, 1), 4 * c + 4):
            z_copy(k, j).start()

    z_start(0, 0)
    z_start(0, 1)
    rows_t[0, 0:CAP, :] = send_t[0:CAP, :]

    same_group = (sub // GROUP) == (lane // GROUP)
    votes = jnp.where((column(clu_row[...]) == clu_row[...]) & same_group, 1.0, 0.0)
    agree_row = jnp.sum(votes, axis=0, keepdims=True)
    agree_col = jnp.sum(votes, axis=1, keepdims=True)
    mean_row = jnp.sum(jnp.where(same_group, agree_col, 0.0), axis=0, keepdims=True) * (1.0 / GROUP)
    own = 2 * (y * NE + e) + sub // (TOK // 2)
    adv = jnp.sum(jnp.where(lane == own, agree_row - mean_row, 0.0), axis=1, keepdims=True)
    weight = column(weight_row[...])
    load_c.wait()
    cot = ((adv * weight) * out_grad[...].astype(F32)).astype(BF16)
    send_c[...] = dot_nn(pick, cot).astype(BF16)
    rows_c[0, 0:CAP, :] = send_c[0:CAP, :]

    def ag_copies(k, c):
        buf = (rows_t, rows_c)[k]
        lo = pl.ds(c * CROWS, CROWS)
        a = pl.ds(c * CROWS, CROWS // 2)
        b = pl.ds(c * CROWS + CROWS // 2, CROWS // 2)
        s, r = ag_ssem, ag_rsem
        return (
            remote(buf.at[0, lo], buf.at[3, lo], s.at[k, c, 0], r.at[k, c, 0], x_next),
            remote(buf.at[0, lo], buf.at[1, lo], s.at[k, c, 1], r.at[k, c, 1], x_prev),
            remote(buf.at[3, a], buf.at[2, a], s.at[k, c, 2], r.at[k, c, 2], x_next),
            remote(buf.at[1, b], buf.at[2, b], s.at[k, c, 3], r.at[k, c, 3], x_prev),
        )

    def ag_send(k, c):
        for j in range(max(4 * c, 1), 4 * c + 4):
            z_copy(k, j).wait_recv()
        for copy in ag_copies(k, c)[:2]:
            copy.start()

    def ag_forward(k, c):
        copies = ag_copies(k, c)
        copies[0].wait_recv()
        copies[2].start()
        copies[1].wait_recv()
        copies[3].start()

    def ag_wait(k, c):
        for copy in ag_copies(k, c)[2:]:
            copy.wait_recv()

    def hrows(m):
        return pl.ds(m * HROWS, HROWS)

    def first_layer(m):
        at = hrows(m)
        pre_g = dot_nn(rows_t[0, at, :], wg[0])
        for i in range(1, 4):
            pre_g += dot_nn(rows_t[i, at, :], wg[i])
        slope[at, :] = pre_g
        pre_u = dot_nn(rows_t[0, at, :], wu[0])
        for i in range(1, 4):
            pre_u += dot_nn(rows_t[i, at, :], wu[i])
        pre_g = slope[at, :]
        sig = jax.nn.sigmoid(pre_g)
        act = pre_g * sig
        hidden[at, :] = (act * pre_u).astype(BF16)
        silu[at, :] = act
        slope[at, :] = pre_u * sig * (1.0 + pre_g * (1.0 - sig))

    def second_layer(m):
        @pl.loop(0, 4)
        def _(i):
            part_o[i, hrows(m), :] = dot_nn(hidden[hrows(m), :], wd[i]).astype(BF16)

    def back_hidden(m):
        at = hrows(m)
        grad = dot_nt(rows_c[0, at, :], wd[0])
        for i in range(1, 4):
            grad += dot_nt(rows_c[i, at, :], wd[i])
        gpre[at, 0:HID] = (grad * slope[at, :]).astype(BF16)
        gpre[at, HID:] = (grad * silu[at, :]).astype(BF16)

    part_i = rows_t

    def back_tokens(m):
        @pl.loop(0, 4)
        def _(i):
            part_i[i, hrows(m), :] = (
                dot_nt(gpre[hrows(m), 0:HID], wg[i]) + dot_nt(gpre[hrows(m), HID:], wu[i])
            ).astype(BF16)

    ORDER = (2, 1, 3, 0)

    def weight_grads(k):
        i = (y + ORDER[k] - x + 4) % 4

        @pl.loop(0, 4)
        def _(f):
            at = pl.ds(pl.multiple_of(f * 256, 256), 256)
            g_gu[k, at, :] = dot_tn(rows_t[i, :, at], gpre[...]).astype(BF16)
            g_dn[k, :, at] = dot_tn(hidden[...], rows_c[i, :, at]).astype(BF16)

    def rs_copies(k, m):
        part = (part_o, part_i)[k]
        a, b = pl.ds(m * CROWS, QROWS), pl.ds(m * CROWS + QROWS, QROWS)
        s, r = rs_ssem, rs_rsem
        return (
            remote(part.at[2, a], x_one.at[k, m, 0], s.at[k, m, 0], r.at[k, m, 0], x_next),
            remote(part.at[2, b], x_one.at[k, m, 1], s.at[k, m, 1], r.at[k, m, 1], x_prev),
            remote(part.at[1, b], x_left.at[k, b], s.at[k, m, 2], r.at[k, m, 2], x_next),
            remote(part.at[3, a], x_right.at[k, a], s.at[k, m, 3], r.at[k, m, 3], x_prev),
            remote(part.at[1, a], x_left.at[k, a], s.at[k, m, 4], r.at[k, m, 4], x_next),
            remote(part.at[3, b], x_right.at[k, b], s.at[k, m, 5], r.at[k, m, 5], x_prev),
        )

    def add_into(ref, at, other):
        ref[at] = (ref[at].astype(F32) + other.astype(F32)).astype(BF16)

    def rs_first(k, m):
        for copy in rs_copies(k, m)[:4]:
            copy.start()

    def rs_pass_on(k, m):
        part = (part_o, part_i)[k]
        copies = rs_copies(k, m)
        copies[0].wait_recv()
        add_into(part, (1, pl.ds(m * CROWS, QROWS)), x_one[k, m, 0])
        copies[4].start()
        copies[1].wait_recv()
        add_into(part, (3, pl.ds(m * CROWS + QROWS, QROWS)), x_one[k, m, 1])
        copies[5].start()

    total = (send_t, send_c)

    def zr_copy(k, j):
        at = pl.ds(j * CAP, CAP)
        return remote(
            total[k].at[at], ret.at[k, at], zr_ssem.at[k, j], zr_rsem.at[k, j], from_of(j)
        )

    def rs_last(k, m):
        part = (part_o, part_i)[k]
        for copy in rs_copies(k, m)[2:]:
            copy.wait_recv()
        at = pl.ds(m * CROWS, CROWS)
        total[k][at, :] = (
            part[0, at, :].astype(F32)
            + x_left[k, at, :].astype(F32)
            + x_right[k, at, :].astype(F32)
        ).astype(BF16)
        for j in range(max(m * 4, 1), m * 4 + 4):
            zr_copy(k, j).start()
        if m == 0:
            ret[k, 0:CAP, :] = total[k][0:CAP, :]

    def back(k):
        for j in range(1, NE):
            zr_copy(k, j).wait_recv()
        spread = jnp.where(
            lax.broadcasted_iota(jnp.int32, (TOK, ROWS), 1) == slot_col, 1.0, 0.0
        ).astype(BF16)
        return dot_nn(spread, ret[k])

    def y_copies():
        s, r = y_ssem, y_rsem
        gu_a, gu_b = pl.ds(0, FB // 2), pl.ds(FB // 2, FB // 2)
        dn_a, dn_b = pl.ds(0, HID // 2), pl.ds(HID // 2, HID // 2)
        return (
            (
                remote(g_gu.at[0, gu_a], y_one_gu.at[0], s.at[0], r.at[0], y_next),
                remote(g_dn.at[0, dn_a], y_one_dn.at[0], s.at[1], r.at[1], y_next),
                remote(g_gu.at[0, gu_b], y_one_gu.at[1], s.at[2], r.at[2], y_prev),
                remote(g_dn.at[0, dn_b], y_one_dn.at[1], s.at[3], r.at[3], y_prev),
            ),
            (
                remote(g_gu.at[1, gu_b], y_left_gu.at[gu_b], s.at[4], r.at[4], y_next),
                remote(g_dn.at[1, dn_b], y_left_dn.at[dn_b], s.at[5], r.at[5], y_next),
            ),
            (
                remote(g_gu.at[2, gu_a], y_right_gu.at[gu_a], s.at[6], r.at[6], y_prev),
                remote(g_dn.at[2, dn_a], y_right_dn.at[dn_a], s.at[7], r.at[7], y_prev),
            ),
            (
                remote(g_gu.at[1, gu_a], y_left_gu.at[gu_a], s.at[8], r.at[8], y_next),
                remote(g_dn.at[1, dn_a], y_left_dn.at[dn_a], s.at[9], r.at[9], y_next),
                remote(g_gu.at[2, gu_b], y_right_gu.at[gu_b], s.at[10], r.at[10], y_prev),
                remote(g_dn.at[2, dn_b], y_right_dn.at[dn_b], s.at[11], r.at[11], y_prev),
            ),
        )

    ag_send(0, 0)
    z_start(0, 2)
    ag_send(0, 1)
    z_start(0, 3)
    ag_forward(0, 0)
    ag_send(0, 2)
    z_start(1, 0)
    z_start(1, 1)
    ag_forward(0, 1)
    ag_send(0, 3)
    z_start(1, 2)
    ag_forward(0, 2)
    z_start(1, 3)
    ag_send(1, 0)
    ag_forward(0, 3)
    ag_send(1, 1)
    for load in loads:
        load.wait()
    ag_wait(0, 0)
    ag_wait(0, 1)
    first_layer(0)
    ag_send(1, 2)
    ag_forward(1, 0)
    ag_send(1, 3)
    ag_wait(0, 2)
    ag_wait(0, 3)
    first_layer(1)
    ag_forward(1, 1)
    second_layer(1)
    second_layer(0)
    ag_forward(1, 2)
    ag_wait(1, 0)
    ag_wait(1, 1)
    back_hidden(0)
    ag_forward(1, 3)
    rs_first(0, 3)
    rs_first(0, 2)
    ag_wait(1, 2)
    ag_wait(1, 3)
    back_hidden(1)
    ys = y_copies()
    weight_grads(0)
    for copy in ys[0]:
        copy.start()
    weight_grads(1)
    for copy in ys[1]:
        copy.start()
    rs_pass_on(0, 3)
    rs_first(0, 1)
    weight_grads(2)
    for copy in ys[2]:
        copy.start()
    rs_pass_on(0, 2)
    rs_first(0, 0)
    weight_grads(3)
    for c in range(CH):
        for copy in ag_copies(0, c):
            copy.wait_send()
    back_tokens(1)
    rs_first(1, 3)
    rs_pass_on(0, 1)
    back_tokens(0)
    rs_pass_on(0, 0)
    rs_first(1, 2)
    for k in range(2):
        for j in range(1, NE):
            z_copy(k, j).wait_send()
    rs_last(0, 3)
    rs_last(0, 2)
    rs_pass_on(1, 3)
    rs_first(1, 1)
    for copy in ys[0]:
        copy.wait_recv()
    FH, HH = FB // 2, HID // 2
    add_into(g_gu, (1, pl.ds(0, FH)), y_one_gu[0])
    add_into(g_dn, (1, pl.ds(0, HH)), y_one_dn[0])
    ys[3][0].start()
    ys[3][1].start()
    add_into(g_gu, (2, pl.ds(FH, FH)), y_one_gu[1])
    add_into(g_dn, (2, pl.ds(HH, HH)), y_one_dn[1])
    ys[3][2].start()
    ys[3][3].start()
    rs_last(0, 1)
    rs_pass_on(1, 2)
    rs_first(1, 0)
    rs_last(0, 0)
    rs_last(1, 3)
    rs_pass_on(1, 1)
    rs_last(1, 2)
    rs_pass_on(1, 0)
    rs_last(1, 1)
    rs_last(1, 0)
    mixed[...] = (weight * back(0).astype(BF16).astype(F32)).astype(BF16)
    grad_tokens[...] = back(1).astype(BF16)
    for copy in ys[1] + ys[2] + ys[3]:
        copy.wait_recv()
    both = (
        g_gu[3].astype(F32) + y_left_gu[...].astype(F32) + y_right_gu[...].astype(F32)
    ).astype(BF16)
    out_gate[0] = both[:, :HID]
    out_up[0] = both[:, HID:]
    out_down[0] = (
        g_dn[3].astype(F32) + y_left_dn[...].astype(F32) + y_right_dn[...].astype(F32)
    ).astype(BF16)

    for c in range(CH):
        for copy in ag_copies(1, c):
            copy.wait_send()
    for k in range(2):
        for m in range(CH):
            for copy in rs_copies(k, m):
                copy.wait_send()
        for j in range(1, NE):
            zr_copy(k, j).wait_send()
    for group in ys:
        for copy in group:
            copy.wait_send()


def finish_kernel(*refs):
    n = len(refs) // 2
    sem = refs[-1]
    copies = [pltpu.make_async_copy(refs[i], refs[n + i], sem.at[i]) for i in range(n)]
    for copy in copies:
        copy.start()
    for copy in copies:
        copy.wait()


def finish(*parts):
    far = pl.BlockSpec(memory_space=pl.ANY)
    return pl.pallas_call(
        finish_kernel,
        out_shape=tuple(jax.ShapeDtypeStruct(p.shape, p.dtype) for p in parts),
        in_specs=[pl.BlockSpec(memory_space=pltpu.VMEM)] * len(parts),
        out_specs=(far,) * len(parts),
        scratch_shapes=[pltpu.SemaphoreType.DMA((len(parts),))],
        compiler_params=pltpu.CompilerParams(vmem_limit_bytes=2**20),
        name="hand_over",
    )(*parts)


def body(tokens, expert_id, route_weight, cluster_id, out_grad, w_gate, w_up, w_down):
    vmem, far = pl.BlockSpec(memory_space=pltpu.VMEM), pl.BlockSpec(memory_space=pl.ANY)
    dma = pltpu.SemaphoreType.DMA
    rollouts = cluster_id.shape[0]
    parts = pl.pallas_call(
        kernel,
        out_shape=(
            pltpu.VMEM((TOK, FB), BF16),
            pltpu.VMEM((TOK, FB), BF16),
            pltpu.VMEM((1, FB, HID), BF16),
            pltpu.VMEM((1, FB, HID), BF16),
            pltpu.VMEM((1, HID, FB), BF16),
        ),
        in_specs=[vmem] * 3 + [far] * 5,
        out_specs=(vmem,) * 5,
        scratch_shapes=[
            pltpu.VMEM((TOK, FB), BF16),
            pltpu.VMEM((TOK, FB), BF16),
            pltpu.VMEM((ROWS, FB), BF16),
            pltpu.VMEM((ROWS, FB), BF16),
            pltpu.VMEM((4, ROWS, FB), BF16),
            pltpu.VMEM((4, ROWS, FB), BF16),
            pltpu.VMEM((4, FB, HID), BF16),
            pltpu.VMEM((4, FB, HID), BF16),
            pltpu.VMEM((4, HID, FB), BF16),
            pltpu.VMEM((ROWS, HID), F32),
            pltpu.VMEM((ROWS, HID), F32),
            pltpu.VMEM((ROWS, HID), BF16),
            pltpu.VMEM((ROWS, 2 * HID), BF16),
            pltpu.VMEM((4, ROWS, FB), BF16),
            pltpu.VMEM((2, CH, 2, QROWS, FB), BF16),
            pltpu.VMEM((2, ROWS, FB), BF16),
            pltpu.VMEM((2, ROWS, FB), BF16),
            pltpu.VMEM((2, ROWS, FB), BF16),
            pltpu.VMEM((4, FB, 2 * HID), BF16),
            pltpu.VMEM((4, HID, FB), BF16),
            pltpu.VMEM((2, FB // 2, 2 * HID), BF16),
            pltpu.VMEM((2, HID // 2, FB), BF16),
            pltpu.VMEM((FB, 2 * HID), BF16),
            pltpu.VMEM((HID, FB), BF16),
            pltpu.VMEM((FB, 2 * HID), BF16),
            pltpu.VMEM((HID, FB), BF16),
            dma((14,)),
            dma((2, NE)),
            dma((2, NE)),
            dma((2, CH, 4)),
            dma((2, CH, 4)),
            dma((2, CH, 6)),
            dma((2, CH, 6)),
            dma((2, NE)),
            dma((2, NE)),
            dma((12,)),
            dma((12,)),
        ],
        compiler_params=pltpu.CompilerParams(
            collective_id=0, has_side_effects=True, vmem_limit_bytes=LIMIT * 2**20
        ),
        name="expert_layer",
    )(
        expert_id.reshape(1, TOK),
        route_weight.reshape(1, TOK),
        cluster_id.reshape(1, rollouts),
        tokens,
        out_grad,
        w_gate,
        w_up,
        w_down,
    )
    return finish(*parts)


def solution(mesh):
    placed = (
        P(("rep", "exp"), "tp"),
        P(("rep", "exp"), None),
        P(("rep", "exp"), None),
        P(),
        P(("rep", "exp"), "tp"),
        P("exp", None, "tp"),
        P("exp", None, "tp"),
        P("exp", "tp", None),
    )
    return jax.shard_map(
        body,
        mesh=mesh,
        in_specs=placed,
        out_specs=(
            P(("rep", "exp"), "tp"),
            P(("rep", "exp"), "tp"),
            P("exp", "rep", "tp"),
            P("exp", "rep", "tp"),
            P("exp", "tp", "rep"),
        ),
        check_vma=False,
    )
```

```python
import jax
import jax.numpy as jnp
from jax import lax
from jax.experimental import pallas as pl
from jax.experimental.pallas import tpu as pltpu
from jax.sharding import PartitionSpec as P

MESH = pl.DeviceIdType.MESH
F32, BF16 = jnp.float32, jnp.bfloat16
TOK = 128
CAP = 32
NE = 16
ROWS = NE * CAP
FB = 1024
HID = 384
GROUP = 16
LIMIT = 56
CH = 4
CROWS = ROWS // CH
HROWS = ROWS // 2
QROWS = CROWS // 2
FAR = (0, 1, 7, 2, 6, 3, 5, 4)


def dot_nn(a, b):
    return lax.dot_general(a, b, (((1,), (0,)), ((), ())), preferred_element_type=F32)


def dot_nt(a, b):
    return lax.dot_general(a, b, (((1,), (1,)), ((), ())), preferred_element_type=F32)


def dot_tn(a, b):
    return lax.dot_general(a, b, (((0,), (0,)), ((), ())), preferred_element_type=F32)


def kernel(
    eid_row,
    weight_row,
    clu_row,
    tokens_far,
    out_grad_far,
    w_gate,
    w_up,
    w_down,
    mixed,
    grad_tokens,
    out_gate,
    out_up,
    out_down,
    tokens,
    out_grad,
    send_t,
    send_c,
    rows_t,
    rows_c,
    wg,
    wu,
    wd,
    wdx,
    slope,
    silu,
    hid,
    gpy,
    rows_y,
    relay,
    acc,
    part_i,
    x_one,
    x_left,
    x_right,
    ret,
    g_dn,
    y_one,
    y_left,
    y_right,
    w_sem,
    z_ssem,
    z_rsem,
    ag_ssem,
    ag_rsem,
    rs_ssem,
    rs_rsem,
    zr_ssem,
    zr_rsem,
    wx_ssem,
    wx_rsem,
    wy_ssem,
    wy_rsem,
    ty_ssem,
    ty_rsem,
    hd_ssem,
    hd_rsem,
    gp_ssem,
    gp_rsem,
    y_ssem,
    y_rsem,
):
    x, y, e = lax.axis_index("tp"), lax.axis_index("rep"), lax.axis_index("exp")
    z, core = e // 2, e % 2
    x_next, x_prev = {"tp": (x + 1) % 4}, {"tp": (x + 3) % 4}
    y_next, y_prev = {"rep": (y + 1) % 4}, {"rep": (y + 3) % 4}
    x_far = {"tp": (x + 2) % 4}

    def to_of(j):
        return {"exp": ((z + FAR[j // 2]) % 8) * 2 + (core + j % 2) % 2}

    def from_of(j):
        return {"exp": ((z + 8 - FAR[j // 2]) % 8) * 2 + (core + j % 2) % 2}

    def remote(src, dst, ssem, rsem, where):
        return pltpu.make_async_remote_copy(
            src_ref=src,
            dst_ref=dst,
            send_sem=ssem,
            recv_sem=rsem,
            device_id=where,
            device_id_type=MESH,
        )

    barrier = pltpu.get_barrier_semaphore()
    for where in [to_of(j) for j in range(1, NE)] + [x_next, x_prev, x_far, y_next, y_prev]:
        pl.semaphore_signal(barrier, inc=1, device_id=where, device_id_type=MESH)
    load_t = pltpu.make_async_copy(tokens_far, tokens, w_sem.at[12])
    load_t.start()
    load_c = pltpu.make_async_copy(out_grad_far, out_grad, w_sem.at[13])
    load_c.start()

    loads, loads_d = [], []
    for i in range(4):
        at = pl.ds(pl.multiple_of(((x + i) % 4) * FB, FB), FB)
        loads.append(pltpu.make_async_copy(w_gate.at[0, at, :], wg.at[i], w_sem.at[i]))
        loads.append(pltpu.make_async_copy(w_up.at[0, at, :], wu.at[i], w_sem.at[4 + i]))
        loads_d.append(pltpu.make_async_copy(w_down.at[0, :, at], wd.at[i], w_sem.at[8 + i]))
    for load in loads_d + loads:
        load.start()

    def place(ids):
        away = ((ids >> 1) - z + 8) & 7
        first = jnp.where(away == 0, 0, jnp.where(away <= 4, 2 * away - 1, 16 - 2 * away))
        return (2 * first + (((ids & 1) + core) & 1)) * CAP

    sub = lax.broadcasted_iota(jnp.int32, (TOK, TOK), 0)
    lane = lax.broadcasted_iota(jnp.int32, (TOK, TOK), 1)

    def column(row):
        return jnp.sum(jnp.where(sub == lane, row, 0), axis=1, keepdims=True)

    ids_row = eid_row[...]
    ids_col = column(ids_row)
    same = ids_col == ids_row
    rank_col = jnp.sum(jnp.where(same & (lane < sub), 1.0, 0.0), axis=1, keepdims=True)
    rank_row = jnp.sum(jnp.where(same & (sub < lane), 1.0, 0.0), axis=0, keepdims=True)
    slot_col = place(ids_col) + rank_col.astype(jnp.int32)
    slot_row = place(ids_row) + rank_row.astype(jnp.int32)
    pick = jnp.where(
        lax.broadcasted_iota(jnp.int32, (ROWS, TOK), 0) == slot_row, 1.0, 0.0
    ).astype(BF16)
    load_t.wait()
    send_t[...] = dot_nn(pick, tokens[...]).astype(BF16)

    pl.semaphore_wait(barrier, NE - 1 + 5)

    def z_copy(k, j):
        src, dst = ((send_t, rows_t), (send_c, rows_c))[k]
        at = pl.ds(j * CAP, CAP)
        return remote(src.at[at], dst.at[0, at], z_ssem.at[k, j], z_rsem.at[k, j], to_of(j))

    def z_start(k, c):
        for j in range(max(4 * c, 1), 4 * c + 4):
            z_copy(k, j).start()

    z_start(0, 0)
    z_start(0, 1)
    rows_t[0, 0:CAP, :] = send_t[0:CAP, :]

    same_group = (sub // GROUP) == (lane // GROUP)
    votes = jnp.where((column(clu_row[...]) == clu_row[...]) & same_group, 1.0, 0.0)
    agree_row = jnp.sum(votes, axis=0, keepdims=True)
    agree_col = jnp.sum(votes, axis=1, keepdims=True)
    mean_row = jnp.sum(jnp.where(same_group, agree_col, 0.0), axis=0, keepdims=True) * (1.0 / GROUP)
    own = 2 * (y * NE + e) + sub // (TOK // 2)
    adv = jnp.sum(jnp.where(lane == own, agree_row - mean_row, 0.0), axis=1, keepdims=True)
    weight = column(weight_row[...])
    load_c.wait()
    cot = ((adv * weight) * out_grad[...].astype(F32)).astype(BF16)
    send_c[...] = dot_nn(pick, cot).astype(BF16)
    rows_c[0, 0:CAP, :] = send_c[0:CAP, :]

    def ring(buf, first, count, ssem, rsem, where, nxt, prv):
        lo = pl.ds(first, count)
        a, b = pl.ds(first, count // 2), pl.ds(first + count // 2, count // 2)
        s, r = [ssem.at[*where, n] for n in range(4)], [rsem.at[*where, n] for n in range(4)]
        return (
            remote(buf.at[0, lo], buf.at[3, lo], s[0], r[0], nxt),
            remote(buf.at[0, lo], buf.at[1, lo], s[1], r[1], prv),
            remote(buf.at[3, a], buf.at[2, a], s[2], r[2], nxt),
            remote(buf.at[1, b], buf.at[2, b], s[3], r[3], prv),
        )

    def ag_copies(k, c):
        buf = (rows_t, rows_c)[k]
        return ring(buf, c * CROWS, CROWS, ag_ssem, ag_rsem, (k, c), x_next, x_prev)

    def hd_copies(m):
        return ring(hid, m * HROWS, HROWS, hd_ssem, hd_rsem, (m,), x_next, x_prev)

    def gp_copies(m):
        return ring(gpy, m * HROWS, HROWS, gp_ssem, gp_rsem, (m,), y_next, y_prev)

    def begin(copies):
        for copy in copies[:2]:
            copy.start()

    def forward(copies):
        copies[0].wait_recv()
        copies[2].start()
        copies[1].wait_recv()
        copies[3].start()

    def ag_send(k, c):
        for j in range(max(4 * c, 1), 4 * c + 4):
            z_copy(k, j).wait_recv()
        for copy in ag_copies(k, c)[:2]:
            copy.start()

    def ag_forward(k, c):
        forward(ag_copies(k, c))

    def ag_wait(k, c):
        for copy in ag_copies(k, c)[2:]:
            copy.wait_recv()

    def hrows(m):
        return pl.ds(m * HROWS, HROWS)

    def first_layer(m):
        at = hrows(m)
        pre_g = dot_nn(rows_t[0, at, :], wg[0])
        for i in range(1, 4):
            pre_g += dot_nn(rows_t[i, at, :], wg[i])
        slope[at, :] = pre_g
        pre_u = dot_nn(rows_t[0, at, :], wu[0])
        for i in range(1, 4):
            pre_u += dot_nn(rows_t[i, at, :], wu[i])
        pre_g = slope[at, :]
        sig = jax.nn.sigmoid(pre_g)
        act = pre_g * sig
        hid[0, at, :] = (act * pre_u).astype(BF16)
        silu[at, :] = act
        slope[at, :] = pre_u * sig * (1.0 + pre_g * (1.0 - sig))

    QD = HID // 4

    def quarter(k, half=None):
        first = ((y + k) % 4) * QD
        if half is None:
            return pl.ds(pl.multiple_of(first, QD), QD)
        return pl.ds(pl.multiple_of(first + half * (QD // 2), QD // 2), QD // 2)

    def wx_copies():
        return [
            remote(
                wd.at[i, quarter(0)], wdx.at[3 - i, quarter(0)], wx_ssem.at[i - 1], wx_rsem.at[i - 1], where
            )
            for i, where in ((1, x_next), (2, x_far), (3, x_prev))
        ]

    def wy_copy(n, at, where):
        return remote(wdx.at[:, at], wdx.at[:, at], wy_ssem.at[n], wy_rsem.at[n], where)

    def wy_sends():
        return (
            wy_copy(0, quarter(0), y_next),
            wy_copy(1, quarter(0), y_prev),
            wy_copy(2, quarter(3, 0), y_next),
            wy_copy(3, quarter(1, 1), y_prev),
        )

    def wy_recvs():
        return (
            wy_copy(0, quarter(3), y_next),
            wy_copy(1, quarter(1), y_prev),
            wy_copy(2, quarter(2, 0), y_next),
            wy_copy(3, quarter(2, 1), y_prev),
        )

    def block(k):
        return (y + k - x + 4) % 4

    def ty_copies(m):
        lo = hrows(m)
        a, b = pl.ds(m * HROWS, HROWS // 2), pl.ds(m * HROWS + HROWS // 2, HROWS // 2)
        s, r = ty_ssem, ty_rsem
        return (
            remote(rows_t.at[block(2), a], relay.at[m, 0], s.at[m, 0], r.at[m, 0], y_next),
            remote(rows_t.at[block(2), b], relay.at[m, 1], s.at[m, 1], r.at[m, 1], y_prev),
            remote(rows_t.at[block(1), lo], rows_y.at[2, lo], s.at[m, 2], r.at[m, 2], y_next),
            remote(rows_t.at[block(3), lo], rows_y.at[0, lo], s.at[m, 3], r.at[m, 3], y_prev),
            remote(relay.at[m, 0], rows_y.at[1, a], s.at[m, 4], r.at[m, 4], y_next),
            remote(relay.at[m, 1], rows_y.at[1, b], s.at[m, 5], r.at[m, 5], y_prev),
        )

    def ty_first(m):
        for copy in ty_copies(m)[:4]:
            copy.start()

    def ty_forward(m):
        copies = ty_copies(m)
        for n in range(2):
            copies[n].wait_recv()
            copies[4 + n].start()

    def back_hidden(m):
        at = hrows(m)
        grad = dot_nt(rows_c[0, at, :], wd[0])
        for i in range(1, 4):
            grad += dot_nt(rows_c[i, at, :], wd[i])
        gpy[0, at, 0:HID] = (grad * slope[at, :]).astype(BF16)
        gpy[0, at, HID:] = (grad * silu[at, :]).astype(BF16)

    def back_tokens(m):
        @pl.loop(0, 4)
        def _(i):
            part_i[i, hrows(m), :] = (
                dot_nt(gpy[0, hrows(m), 0:HID], wg[i]) + dot_nt(gpy[0, hrows(m), HID:], wu[i])
            ).astype(BF16)

    ORDER = (2, 1, 3, 0)

    def down_grads(k):
        i = block(ORDER[k])

        @pl.loop(0, 4)
        def _(f):
            at = pl.ds(pl.multiple_of(f * 256, 256), 256)
            g_dn[k, :, at] = dot_tn(hid[0], rows_c[i, :, at]).astype(BF16)

    def gate_up_grads(k, last=False):
        rows = rows_t.at[block(0)] if k == 0 else rows_y.at[k - 1]

        @pl.loop(0, 4)
        def _(f):
            at = pl.ds(pl.multiple_of(f * 256, 256), 256)
            term = dot_tn(rows[:, at], gpy[k])
            if k == 0:
                acc[at, :] = term
            elif not last:
                acc[at, :] += term
            else:
                both = (acc[at, :] + term).astype(BF16)
                out_gate[0, at, :] = both[:, :HID]
                out_up[0, at, :] = both[:, HID:]

    def rs_copies(m):
        a, b = pl.ds(m * CROWS, QROWS), pl.ds(m * CROWS + QROWS, QROWS)
        s, r = rs_ssem, rs_rsem
        return (
            remote(part_i.at[2, a], x_one.at[m, 0], s.at[m, 0], r.at[m, 0], x_next),
            remote(part_i.at[2, b], x_one.at[m, 1], s.at[m, 1], r.at[m, 1], x_prev),
            remote(part_i.at[1, b], x_left.at[b], s.at[m, 2], r.at[m, 2], x_next),
            remote(part_i.at[3, a], x_right.at[a], s.at[m, 3], r.at[m, 3], x_prev),
            remote(part_i.at[1, a], x_left.at[a], s.at[m, 4], r.at[m, 4], x_next),
            remote(part_i.at[3, b], x_right.at[b], s.at[m, 5], r.at[m, 5], x_prev),
        )

    def add_into(ref, at, other):
        ref[at] = (ref[at].astype(F32) + other.astype(F32)).astype(BF16)

    def rs_first(m):
        for copy in rs_copies(m)[:4]:
            copy.start()

    def rs_pass_on(m):
        copies = rs_copies(m)
        copies[0].wait_recv()
        add_into(part_i, (1, pl.ds(m * CROWS, QROWS)), x_one[m, 0])
        copies[4].start()
        copies[1].wait_recv()
        add_into(part_i, (3, pl.ds(m * CROWS + QROWS, QROWS)), x_one[m, 1])
        copies[5].start()

    total = (send_t, send_c)

    def zr_copy(k, j):
        at = pl.ds(j * CAP, CAP)
        return remote(
            total[k].at[at], ret.at[k, at], zr_ssem.at[k, j], zr_rsem.at[k, j], from_of(j)
        )

    def zr_start(k, m):
        for j in range(max(m * 4, 1), m * 4 + 4):
            zr_copy(k, j).start()
        if m == 0:
            ret[k, 0:CAP, :] = total[k][0:CAP, :]

    def rs_last(m):
        for copy in rs_copies(m)[2:]:
            copy.wait_recv()
        at = pl.ds(m * CROWS, CROWS)
        total[1][at, :] = (
            part_i[0, at, :].astype(F32) + x_left[at, :].astype(F32) + x_right[at, :].astype(F32)
        ).astype(BF16)
        zr_start(1, m)

    def second_layer(m):
        for copy in hd_copies(m)[2:]:
            copy.wait_recv()
        at = hrows(m)
        out = dot_nn(hid[0, at, :], wd[0])
        for i in range(1, 4):
            out += dot_nn(hid[i, at, :], wdx[i - 1])
        total[0][at, :] = out.astype(BF16)
        zr_start(0, 2 * m + 1)
        zr_start(0, 2 * m)

    def back(k):
        for j in range(1, NE):
            zr_copy(k, j).wait_recv()
        spread = jnp.where(
            lax.broadcasted_iota(jnp.int32, (TOK, ROWS), 1) == slot_col, 1.0, 0.0
        ).astype(BF16)
        return dot_nn(spread, ret[k])

    HH = HID // 2
    dn_a, dn_b = pl.ds(0, HH), pl.ds(HH, HH)

    def y_copies():
        s, r = y_ssem, y_rsem
        return (
            remote(g_dn.at[0, dn_a], y_one.at[0], s.at[0], r.at[0], y_next),
            remote(g_dn.at[0, dn_b], y_one.at[1], s.at[1], r.at[1], y_prev),
            remote(g_dn.at[1, dn_b], y_left.at[dn_b], s.at[2], r.at[2], y_next),
            remote(g_dn.at[2, dn_a], y_right.at[dn_a], s.at[3], r.at[3], y_prev),
            remote(g_dn.at[1, dn_a], y_left.at[dn_a], s.at[4], r.at[4], y_next),
            remote(g_dn.at[2, dn_b], y_right.at[dn_b], s.at[5], r.at[5], y_prev),
        )

    for load in loads_d:
        load.wait()
    for copy in wx_copies():
        copy.start()
    ag_send(0, 0)
    z_start(0, 2)
    ag_send(0, 1)
    z_start(0, 3)
    ag_forward(0, 0)
    ag_send(0, 2)
    z_start(1, 0)
    z_start(1, 1)
    for copy in wx_copies():
        copy.wait_recv()
    begin(wy_sends())
    ag_forward(0, 1)
    ag_send(0, 3)
    z_start(1, 2)
    ag_forward(0, 2)
    z_start(1, 3)
    ag_send(1, 0)
    ag_forward(0, 3)
    ag_send(1, 1)
    for load in loads:
        load.wait()
    ag_wait(0, 0)
    ag_wait(0, 1)
    ty_first(0)
    first_layer(0)
    for n in range(2):
        wy_recvs()[n].wait_recv()
        wy_sends()[2 + n].start()
    ag_send(1, 2)
    ag_forward(1, 0)
    ag_send(1, 3)
    ag_wait(0, 2)
    ag_wait(0, 3)
    ty_first(1)
    first_layer(1)
    ag_forward(1, 1)
    ty_forward(0)
    ag_forward(1, 2)
    ag_wait(1, 0)
    ag_wait(1, 1)
    back_hidden(0)
    begin(gp_copies(0))
    ag_forward(1, 3)
    begin(hd_copies(1))
    begin(hd_copies(0))
    ty_forward(1)
    ag_wait(1, 2)
    ag_wait(1, 3)
    back_hidden(1)
    begin(gp_copies(1))
    ys = y_copies()
    down_grads(0)
    ys[0].start()
    ys[1].start()
    down_grads(1)
    ys[2].start()
    down_grads(2)
    ys[3].start()
    back_tokens(1)
    rs_first(3)
    rs_first(2)
    forward(hd_copies(1))
    forward(hd_copies(0))
    back_tokens(0)
    forward(gp_copies(0))
    rs_pass_on(3)
    rs_first(1)
    for copy in wy_recvs()[2:]:
        copy.wait_recv()
    for k in range(2):
        for j in range(1, NE):
            z_copy(k, j).wait_send()
    second_layer(1)
    rs_pass_on(2)
    rs_first(0)
    second_layer(0)
    forward(gp_copies(1))
    ys[0].wait_recv()
    add_into(g_dn, (1, dn_a), y_one[0])
    ys[4].start()
    ys[1].wait_recv()
    add_into(g_dn, (2, dn_b), y_one[1])
    ys[5].start()
    gate_up_grads(0)
    rs_pass_on(1)
    rs_last(3)
    for m in range(2):
        ty_copies(m)[2].wait_recv()
        ty_copies(m)[3].wait_recv()
    gate_up_grads(3)
    rs_pass_on(0)
    rs_last(2)
    gate_up_grads(1)
    down_grads(3)
    rs_last(1)
    rs_last(0)
    mixed[...] = (weight * back(0).astype(BF16).astype(F32)).astype(BF16)
    for m in range(2):
        ty_copies(m)[4].wait_recv()
        ty_copies(m)[5].wait_recv()
        gp_copies(m)[2].wait_recv()
        gp_copies(m)[3].wait_recv()
    gate_up_grads(2, last=True)
    for copy in ys[2:]:
        copy.wait_recv()
    out_down[0] = (
        g_dn[3].astype(F32) + y_left[...].astype(F32) + y_right[...].astype(F32)
    ).astype(BF16)
    grad_tokens[...] = back(1).astype(BF16)

    for k in range(2):
        for c in range(CH):
            for copy in ag_copies(k, c):
                copy.wait_send()
        for copy in ty_copies(k) + hd_copies(k) + gp_copies(k):
            copy.wait_send()
        for j in range(1, NE):
            zr_copy(k, j).wait_send()
    for m in range(CH):
        for copy in rs_copies(m):
            copy.wait_send()
    for copy in wx_copies() + list(wy_sends()) + list(ys):
        copy.wait_send()


def finish_kernel(*refs):
    n = len(refs) // 2
    sem = refs[-1]
    copies = [pltpu.make_async_copy(refs[i], refs[n + i], sem.at[i]) for i in range(n)]
    for copy in copies:
        copy.start()
    for copy in copies:
        copy.wait()


def finish(*parts):
    far = pl.BlockSpec(memory_space=pl.ANY)
    return pl.pallas_call(
        finish_kernel,
        out_shape=tuple(jax.ShapeDtypeStruct(p.shape, p.dtype) for p in parts),
        in_specs=[pl.BlockSpec(memory_space=pltpu.VMEM)] * len(parts),
        out_specs=(far,) * len(parts),
        scratch_shapes=[pltpu.SemaphoreType.DMA((len(parts),))],
        compiler_params=pltpu.CompilerParams(vmem_limit_bytes=2**20),
        name="hand_over",
    )(*parts)


def body(tokens, expert_id, route_weight, cluster_id, out_grad, w_gate, w_up, w_down):
    vmem, far = pl.BlockSpec(memory_space=pltpu.VMEM), pl.BlockSpec(memory_space=pl.ANY)
    dma = pltpu.SemaphoreType.DMA
    rollouts = cluster_id.shape[0]
    parts = pl.pallas_call(
        kernel,
        out_shape=(
            pltpu.VMEM((TOK, FB), BF16),
            pltpu.VMEM((TOK, FB), BF16),
            pltpu.VMEM((1, FB, HID), BF16),
            pltpu.VMEM((1, FB, HID), BF16),
            pltpu.VMEM((1, HID, FB), BF16),
        ),
        in_specs=[vmem] * 3 + [far] * 5,
        out_specs=(vmem,) * 5,
        scratch_shapes=[
            pltpu.VMEM((TOK, FB), BF16),
            pltpu.VMEM((TOK, FB), BF16),
            pltpu.VMEM((ROWS, FB), BF16),
            pltpu.VMEM((ROWS, FB), BF16),
            pltpu.VMEM((4, ROWS, FB), BF16),
            pltpu.VMEM((4, ROWS, FB), BF16),
            pltpu.VMEM((4, FB, HID), BF16),
            pltpu.VMEM((4, FB, HID), BF16),
            pltpu.VMEM((4, HID, FB), BF16),
            pltpu.VMEM((3, HID, FB), BF16),
            pltpu.VMEM((ROWS, HID), F32),
            pltpu.VMEM((ROWS, HID), F32),
            pltpu.VMEM((4, ROWS, HID), BF16),
            pltpu.VMEM((4, ROWS, 2 * HID), BF16),
            pltpu.VMEM((3, ROWS, FB), BF16),
            pltpu.VMEM((2, 2, HROWS // 2, FB), BF16),
            pltpu.VMEM((FB, 2 * HID), F32),
            pltpu.VMEM((4, ROWS, FB), BF16),
            pltpu.VMEM((CH, 2, QROWS, FB), BF16),
            pltpu.VMEM((ROWS, FB), BF16),
            pltpu.VMEM((ROWS, FB), BF16),
            pltpu.VMEM((2, ROWS, FB), BF16),
            pltpu.VMEM((4, HID, FB), BF16),
            pltpu.VMEM((2, HID // 2, FB), BF16),
            pltpu.VMEM((HID, FB), BF16),
            pltpu.VMEM((HID, FB), BF16),
            dma((14,)),
            dma((2, NE)),
            dma((2, NE)),
            dma((2, CH, 4)),
            dma((2, CH, 4)),
            dma((CH, 6)),
            dma((CH, 6)),
            dma((2, NE)),
            dma((2, NE)),
            dma((3,)),
            dma((3,)),
            dma((4,)),
            dma((4,)),
            dma((2, 6)),
            dma((2, 6)),
            dma((2, 4)),
            dma((2, 4)),
            dma((2, 4)),
            dma((2, 4)),
            dma((6,)),
            dma((6,)),
        ],
        compiler_params=pltpu.CompilerParams(
            collective_id=0, has_side_effects=True, vmem_limit_bytes=LIMIT * 2**20
        ),
        name="expert_layer",
    )(
        expert_id.reshape(1, TOK),
        route_weight.reshape(1, TOK),
        cluster_id.reshape(1, rollouts),
        tokens,
        out_grad,
        w_gate,
        w_up,
        w_down,
    )
    return finish(*parts)


def solution(mesh):
    placed = (
        P(("rep", "exp"), "tp"),
        P(("rep", "exp"), None),
        P(("rep", "exp"), None),
        P(),
        P(("rep", "exp"), "tp"),
        P("exp", None, "tp"),
        P("exp", None, "tp"),
        P("exp", "tp", None),
    )
    return jax.shard_map(
        body,
        mesh=mesh,
        in_specs=placed,
        out_specs=(
            P(("rep", "exp"), "tp"),
            P(("rep", "exp"), "tp"),
            P("exp", "rep", "tp"),
            P("exp", "rep", "tp"),
            P("exp", "tp", "rep"),
        ),
        check_vma=False,
    )
```

```python
import jax
import jax.numpy as jnp
from jax import lax
from jax.experimental import pallas as pl
from jax.experimental.pallas import tpu as pltpu
from jax.sharding import PartitionSpec as P

MESH = pl.DeviceIdType.MESH
F32, BF16 = jnp.float32, jnp.bfloat16
TOK = 128
CAP = 32
NE = 16
ROWS = NE * CAP
FB = 1024
HID = 384
GROUP = 16
LIMIT = 56
CH = 4
CROWS = ROWS // CH
HROWS = ROWS // 2
QROWS = CROWS // 2
FAR = (0, 1, 3, 5, 4, 7, 2, 6)


def dot_nn(a, b):
    return lax.dot_general(a, b, (((1,), (0,)), ((), ())), preferred_element_type=F32)


def dot_nt(a, b):
    return lax.dot_general(a, b, (((1,), (1,)), ((), ())), preferred_element_type=F32)


def dot_tn(a, b):
    return lax.dot_general(a, b, (((0,), (0,)), ((), ())), preferred_element_type=F32)


def kernel(
    eid_row,
    weight_row,
    clu_row,
    tokens_far,
    out_grad_far,
    w_gate,
    w_up,
    w_down,
    mixed,
    grad_tokens,
    out_gate,
    out_up,
    out_down,
    tokens,
    out_grad,
    send_t,
    send_c,
    rows_t,
    rows_c,
    wg,
    wu,
    wd,
    wdx,
    slope,
    silu,
    hid,
    gpy,
    rows_y,
    relay,
    acc,
    part_i,
    x_one,
    x_left,
    x_right,
    ret,
    g_dn,
    y_one,
    y_left,
    y_right,
    w_sem,
    z_ssem,
    z_rsem,
    ag_ssem,
    ag_rsem,
    rs_ssem,
    rs_rsem,
    zr_ssem,
    zr_rsem,
    wx_ssem,
    wx_rsem,
    wy_ssem,
    wy_rsem,
    ty_ssem,
    ty_rsem,
    hd_ssem,
    hd_rsem,
    gp_ssem,
    gp_rsem,
    y_ssem,
    y_rsem,
):
    x, y, e = lax.axis_index("tp"), lax.axis_index("rep"), lax.axis_index("exp")
    z, core = e // 2, e % 2
    x_next, x_prev = {"tp": (x + 1) % 4}, {"tp": (x + 3) % 4}
    y_next, y_prev = {"rep": (y + 1) % 4}, {"rep": (y + 3) % 4}
    x_far = {"tp": (x + 2) % 4}

    def to_of(j):
        return {"exp": ((z + FAR[j // 2]) % 8) * 2 + (core + j % 2) % 2}

    def from_of(j):
        return {"exp": ((z + 8 - FAR[j // 2]) % 8) * 2 + (core + j % 2) % 2}

    def remote(src, dst, ssem, rsem, where):
        return pltpu.make_async_remote_copy(
            src_ref=src,
            dst_ref=dst,
            send_sem=ssem,
            recv_sem=rsem,
            device_id=where,
            device_id_type=MESH,
        )

    barrier = pltpu.get_barrier_semaphore()
    for where in [to_of(j) for j in range(1, NE)] + [x_next, x_prev, x_far, y_next, y_prev]:
        pl.semaphore_signal(barrier, inc=1, device_id=where, device_id_type=MESH)
    load_t = pltpu.make_async_copy(tokens_far, tokens, w_sem.at[12])
    load_t.start()
    load_c = pltpu.make_async_copy(out_grad_far, out_grad, w_sem.at[13])
    load_c.start()

    loads, loads_d = [], []
    for i in range(4):
        at = pl.ds(pl.multiple_of(((x + i) % 4) * FB, FB), FB)
        loads.append(pltpu.make_async_copy(w_gate.at[0, at, :], wg.at[i], w_sem.at[i]))
        loads.append(pltpu.make_async_copy(w_up.at[0, at, :], wu.at[i], w_sem.at[4 + i]))
        loads_d.append(pltpu.make_async_copy(w_down.at[0, :, at], wd.at[i], w_sem.at[8 + i]))
    for load in loads_d + loads:
        load.start()

    def place(ids):
        away = ((ids >> 1) - z + 8) & 7
        first = sum(jnp.where(away == far, n, 0) for n, far in enumerate(FAR))
        return (2 * first + (((ids & 1) + core) & 1)) * CAP

    sub = lax.broadcasted_iota(jnp.int32, (TOK, TOK), 0)
    lane = lax.broadcasted_iota(jnp.int32, (TOK, TOK), 1)

    def column(row):
        return jnp.sum(jnp.where(sub == lane, row, 0), axis=1, keepdims=True)

    ids_row = eid_row[...]
    ids_col = column(ids_row)
    same = ids_col == ids_row
    rank_col = jnp.sum(jnp.where(same & (lane < sub), 1.0, 0.0), axis=1, keepdims=True)
    rank_row = jnp.sum(jnp.where(same & (sub < lane), 1.0, 0.0), axis=0, keepdims=True)
    slot_col = place(ids_col) + rank_col.astype(jnp.int32)
    slot_row = place(ids_row) + rank_row.astype(jnp.int32)
    pick = jnp.where(
        lax.broadcasted_iota(jnp.int32, (ROWS, TOK), 0) == slot_row, 1.0, 0.0
    ).astype(BF16)
    load_t.wait()
    send_t[...] = dot_nn(pick, tokens[...]).astype(BF16)

    pl.semaphore_wait(barrier, NE - 1 + 5)

    def z_copy(k, j):
        src, dst = ((send_t, rows_t), (send_c, rows_c))[k]
        at = pl.ds(j * CAP, CAP)
        return remote(src.at[at], dst.at[0, at], z_ssem.at[k, j], z_rsem.at[k, j], to_of(j))

    def z_start(k, c):
        for j in range(max(4 * c, 1), 4 * c + 4):
            z_copy(k, j).start()

    z_start(0, 0)
    z_start(0, 1)
    rows_t[0, 0:CAP, :] = send_t[0:CAP, :]

    same_group = (sub // GROUP) == (lane // GROUP)
    votes = jnp.where((column(clu_row[...]) == clu_row[...]) & same_group, 1.0, 0.0)
    agree_row = jnp.sum(votes, axis=0, keepdims=True)
    agree_col = jnp.sum(votes, axis=1, keepdims=True)
    mean_row = jnp.sum(jnp.where(same_group, agree_col, 0.0), axis=0, keepdims=True) * (1.0 / GROUP)
    own = 2 * (y * NE + e) + sub // (TOK // 2)
    adv = jnp.sum(jnp.where(lane == own, agree_row - mean_row, 0.0), axis=1, keepdims=True)
    weight = column(weight_row[...])
    load_c.wait()
    cot = ((adv * weight) * out_grad[...].astype(F32)).astype(BF16)
    send_c[...] = dot_nn(pick, cot).astype(BF16)
    rows_c[0, 0:CAP, :] = send_c[0:CAP, :]

    def ring(buf, first, count, ssem, rsem, where, nxt, prv):
        lo = pl.ds(first, count)
        a, b = pl.ds(first, count // 2), pl.ds(first + count // 2, count // 2)
        s, r = [ssem.at[*where, n] for n in range(4)], [rsem.at[*where, n] for n in range(4)]
        return (
            remote(buf.at[0, lo], buf.at[3, lo], s[0], r[0], nxt),
            remote(buf.at[0, lo], buf.at[1, lo], s[1], r[1], prv),
            remote(buf.at[3, a], buf.at[2, a], s[2], r[2], nxt),
            remote(buf.at[1, b], buf.at[2, b], s[3], r[3], prv),
        )

    def ag_copies(k, c):
        buf = (rows_t, rows_c)[k]
        return ring(buf, c * CROWS, CROWS, ag_ssem, ag_rsem, (k, c), x_next, x_prev)

    def hd_copies(m):
        return ring(hid, m * HROWS, HROWS, hd_ssem, hd_rsem, (m,), x_next, x_prev)

    def gp_copies(m):
        return ring(gpy, m * HROWS, HROWS, gp_ssem, gp_rsem, (m,), y_next, y_prev)

    def begin(copies):
        for copy in copies[:2]:
            copy.start()

    def forward(copies):
        copies[0].wait_recv()
        copies[2].start()
        copies[1].wait_recv()
        copies[3].start()

    def ag_send(k, c):
        for j in range(max(4 * c, 1), 4 * c + 4):
            z_copy(k, j).wait_recv()
        for copy in ag_copies(k, c)[:2]:
            copy.start()

    def ag_forward(k, c):
        forward(ag_copies(k, c))

    def ag_wait(k, c):
        for copy in ag_copies(k, c)[2:]:
            copy.wait_recv()

    def hrows(m):
        return pl.ds(m * HROWS, HROWS)

    def first_layer(m):
        at = hrows(m)
        pre_g = dot_nn(rows_t[0, at, :], wg[0])
        for i in range(1, 4):
            pre_g += dot_nn(rows_t[i, at, :], wg[i])
        slope[at, :] = pre_g
        pre_u = dot_nn(rows_t[0, at, :], wu[0])
        for i in range(1, 4):
            pre_u += dot_nn(rows_t[i, at, :], wu[i])
        pre_g = slope[at, :]
        sig = jax.nn.sigmoid(pre_g)
        act = pre_g * sig
        hid[0, at, :] = (act * pre_u).astype(BF16)
        silu[at, :] = act
        slope[at, :] = pre_u * sig * (1.0 + pre_g * (1.0 - sig))

    QD = HID // 4

    def quarter(k, half=None):
        first = ((y + k) % 4) * QD
        if half is None:
            return pl.ds(pl.multiple_of(first, QD), QD)
        return pl.ds(pl.multiple_of(first + half * (QD // 2), QD // 2), QD // 2)

    def wx_copies():
        return [
            remote(
                wd.at[i, quarter(0)], wdx.at[3 - i, quarter(0)], wx_ssem.at[i - 1], wx_rsem.at[i - 1], where
            )
            for i, where in ((1, x_next), (2, x_far), (3, x_prev))
        ]

    def wy_copy(n, at, where):
        return remote(wdx.at[:, at], wdx.at[:, at], wy_ssem.at[n], wy_rsem.at[n], where)

    def wy_sends():
        return (
            wy_copy(0, quarter(0), y_next),
            wy_copy(1, quarter(0), y_prev),
            wy_copy(2, quarter(3, 0), y_next),
            wy_copy(3, quarter(1, 1), y_prev),
        )

    def wy_recvs():
        return (
            wy_copy(0, quarter(3), y_next),
            wy_copy(1, quarter(1), y_prev),
            wy_copy(2, quarter(2, 0), y_next),
            wy_copy(3, quarter(2, 1), y_prev),
        )

    def block(k):
        return (y + k - x + 4) % 4

    def ty_copies(m):
        lo = pl.ds(m * CROWS, CROWS)
        a, b = pl.ds(m * CROWS, QROWS), pl.ds(m * CROWS + QROWS, QROWS)
        s, r = ty_ssem, ty_rsem
        return (
            remote(rows_t.at[block(2), a], relay.at[m, 0], s.at[m, 0], r.at[m, 0], y_next),
            remote(rows_t.at[block(2), b], relay.at[m, 1], s.at[m, 1], r.at[m, 1], y_prev),
            remote(rows_t.at[block(1), lo], rows_y.at[2, lo], s.at[m, 2], r.at[m, 2], y_next),
            remote(rows_t.at[block(3), lo], rows_y.at[0, lo], s.at[m, 3], r.at[m, 3], y_prev),
            remote(relay.at[m, 0], rows_y.at[1, a], s.at[m, 4], r.at[m, 4], y_next),
            remote(relay.at[m, 1], rows_y.at[1, b], s.at[m, 5], r.at[m, 5], y_prev),
        )

    def ty_first(m):
        ag_wait(0, m)
        for copy in ty_copies(m)[:4]:
            copy.start()

    def ty_forward(m):
        copies = ty_copies(m)
        for n in range(2):
            copies[n].wait_recv()
            copies[4 + n].start()

    def back_hidden(m):
        at = hrows(m)
        grad = dot_nt(rows_c[0, at, :], wd[0])
        for i in range(1, 4):
            grad += dot_nt(rows_c[i, at, :], wd[i])
        gpy[0, at, 0:HID] = (grad * slope[at, :]).astype(BF16)
        gpy[0, at, HID:] = (grad * silu[at, :]).astype(BF16)

    def back_tokens(m):
        @pl.loop(0, 4)
        def _(i):
            part_i[i, hrows(m), :] = (
                dot_nt(gpy[0, hrows(m), 0:HID], wg[i]) + dot_nt(gpy[0, hrows(m), HID:], wu[i])
            ).astype(BF16)

    ORDER = (2, 1, 3, 0)

    def down_grads(k):
        i = block(ORDER[k])

        @pl.loop(0, 4)
        def _(f):
            at = pl.ds(pl.multiple_of(f * 256, 256), 256)
            g_dn[k, :, at] = dot_tn(hid[0], rows_c[i, :, at]).astype(BF16)

    def gate_up_grads(k, last=False):
        rows = rows_t.at[block(0)] if k == 0 else rows_y.at[k - 1]

        @pl.loop(0, 4)
        def _(f):
            at = pl.ds(pl.multiple_of(f * 256, 256), 256)
            term = dot_tn(rows[:, at], gpy[k])
            if k == 0:
                acc[at, :] = term
            elif not last:
                acc[at, :] += term
            else:
                both = (acc[at, :] + term).astype(BF16)
                out_gate[0, at, :] = both[:, :HID]
                out_up[0, at, :] = both[:, HID:]

    def rs_copies(m):
        a, b = pl.ds(m * CROWS, QROWS), pl.ds(m * CROWS + QROWS, QROWS)
        s, r = rs_ssem, rs_rsem
        return (
            remote(part_i.at[2, a], x_one.at[m, 0], s.at[m, 0], r.at[m, 0], x_next),
            remote(part_i.at[2, b], x_one.at[m, 1], s.at[m, 1], r.at[m, 1], x_prev),
            remote(part_i.at[1, b], x_left.at[b], s.at[m, 2], r.at[m, 2], x_next),
            remote(part_i.at[3, a], x_right.at[a], s.at[m, 3], r.at[m, 3], x_prev),
            remote(part_i.at[1, a], x_left.at[a], s.at[m, 4], r.at[m, 4], x_next),
            remote(part_i.at[3, b], x_right.at[b], s.at[m, 5], r.at[m, 5], x_prev),
        )

    def add_into(ref, at, other):
        ref[at] = (ref[at].astype(F32) + other.astype(F32)).astype(BF16)

    def rs_first(m):
        for copy in rs_copies(m)[:4]:
            copy.start()

    def rs_pass_on(m):
        copies = rs_copies(m)
        copies[0].wait_recv()
        add_into(part_i, (1, pl.ds(m * CROWS, QROWS)), x_one[m, 0])
        copies[4].start()
        copies[1].wait_recv()
        add_into(part_i, (3, pl.ds(m * CROWS + QROWS, QROWS)), x_one[m, 1])
        copies[5].start()

    total = (send_t, send_c)

    def zr_copy(k, j):
        at = pl.ds(j * CAP, CAP)
        return remote(
            total[k].at[at], ret.at[k, at], zr_ssem.at[k, j], zr_rsem.at[k, j], from_of(j)
        )

    def zr_start(k, m):
        for j in range(max(m * 4, 1), m * 4 + 4):
            zr_copy(k, j).start()
        if m == 0:
            ret[k, 0:CAP, :] = total[k][0:CAP, :]

    def rs_last(m):
        for copy in rs_copies(m)[2:]:
            copy.wait_recv()
        at = pl.ds(m * CROWS, CROWS)
        total[1][at, :] = (
            part_i[0, at, :].astype(F32) + x_left[at, :].astype(F32) + x_right[at, :].astype(F32)
        ).astype(BF16)
        zr_start(1, m)

    def second_layer(m):
        for copy in hd_copies(m)[2:]:
            copy.wait_recv()
        at = hrows(m)
        out = dot_nn(hid[0, at, :], wd[0])
        for i in range(1, 4):
            out += dot_nn(hid[i, at, :], wdx[i - 1])
        total[0][at, :] = out.astype(BF16)
        zr_start(0, 2 * m + 1)
        zr_start(0, 2 * m)

    def back(k):
        for j in range(1, NE):
            zr_copy(k, j).wait_recv()
        spread = jnp.where(
            lax.broadcasted_iota(jnp.int32, (TOK, ROWS), 1) == slot_col, 1.0, 0.0
        ).astype(BF16)
        return dot_nn(spread, ret[k])

    HH = HID // 2
    dn_a, dn_b = pl.ds(0, HH), pl.ds(HH, HH)

    def y_copies():
        s, r = y_ssem, y_rsem
        return (
            remote(g_dn.at[0, dn_a], y_one.at[0], s.at[0], r.at[0], y_next),
            remote(g_dn.at[0, dn_b], y_one.at[1], s.at[1], r.at[1], y_prev),
            remote(g_dn.at[1, dn_b], y_left.at[dn_b], s.at[2], r.at[2], y_next),
            remote(g_dn.at[2, dn_a], y_right.at[dn_a], s.at[3], r.at[3], y_prev),
            remote(g_dn.at[1, dn_a], y_left.at[dn_a], s.at[4], r.at[4], y_next),
            remote(g_dn.at[2, dn_b], y_right.at[dn_b], s.at[5], r.at[5], y_prev),
        )

    for load in loads_d:
        load.wait()
    for copy in wx_copies():
        copy.start()
    ag_send(0, 0)
    z_start(0, 2)
    ag_send(0, 1)
    z_start(0, 3)
    ag_forward(0, 0)
    ag_send(0, 2)
    z_start(1, 0)
    z_start(1, 1)
    for copy in wx_copies():
        copy.wait_recv()
    begin(wy_sends())
    ag_forward(0, 1)
    ty_first(0)
    ag_send(0, 3)
    z_start(1, 2)
    ag_forward(0, 2)
    ty_first(1)
    z_start(1, 3)
    ag_send(1, 0)
    ag_forward(0, 3)
    for n in range(2):
        wy_recvs()[n].wait_recv()
        wy_sends()[2 + n].start()
    ty_first(2)
    ty_forward(0)
    ag_send(1, 1)
    for load in loads:
        load.wait()
    first_layer(0)
    begin(hd_copies(0))
    ag_send(1, 2)
    ag_forward(1, 0)
    ag_send(1, 3)
    ty_first(3)
    ty_forward(1)
    first_layer(1)
    ag_forward(1, 1)
    ty_forward(2)
    forward(hd_copies(0))
    ag_forward(1, 2)
    ag_wait(1, 0)
    ag_wait(1, 1)
    back_hidden(0)
    begin(gp_copies(0))
    for k in range(2):
        for j in range(1, NE):
            z_copy(k, j).wait_send()
    for copy in wy_recvs()[2:]:
        copy.wait_recv()
    second_layer(0)
    ty_forward(3)
    ag_forward(1, 3)
    begin(hd_copies(1))
    ag_wait(1, 2)
    ag_wait(1, 3)
    back_hidden(1)
    begin(gp_copies(1))
    forward(hd_copies(1))
    back_tokens(1)
    rs_first(3)
    rs_first(2)
    ys = y_copies()
    down_grads(0)
    ys[0].start()
    ys[1].start()
    forward(gp_copies(0))
    down_grads(1)
    ys[2].start()
    down_grads(2)
    ys[3].start()
    back_tokens(0)
    rs_pass_on(3)
    rs_first(1)
    second_layer(1)
    rs_pass_on(2)
    rs_first(0)
    gate_up_grads(0)
    forward(gp_copies(1))
    rs_last(3)
    ys[0].wait_recv()
    add_into(g_dn, (1, dn_a), y_one[0])
    ys[4].start()
    ys[1].wait_recv()
    add_into(g_dn, (2, dn_b), y_one[1])
    ys[5].start()
    rs_pass_on(1)
    for m in range(CH):
        ty_copies(m)[2].wait_recv()
        ty_copies(m)[3].wait_recv()
    gate_up_grads(3)
    rs_last(2)
    gate_up_grads(1)
    rs_pass_on(0)
    down_grads(3)
    mixed[...] = (weight * back(0).astype(BF16).astype(F32)).astype(BF16)
    rs_last(1)
    rs_last(0)
    for m in range(CH):
        ty_copies(m)[4].wait_recv()
        ty_copies(m)[5].wait_recv()
    for m in range(2):
        gp_copies(m)[2].wait_recv()
        gp_copies(m)[3].wait_recv()
    gate_up_grads(2, last=True)
    for copy in ys[2:]:
        copy.wait_recv()
    out_down[0] = (
        g_dn[3].astype(F32) + y_left[...].astype(F32) + y_right[...].astype(F32)
    ).astype(BF16)
    grad_tokens[...] = back(1).astype(BF16)

    for k in range(2):
        for c in range(CH):
            for copy in ag_copies(k, c):
                copy.wait_send()
        for copy in hd_copies(k) + gp_copies(k):
            copy.wait_send()
        for j in range(1, NE):
            zr_copy(k, j).wait_send()
    for m in range(CH):
        for copy in ty_copies(m) + rs_copies(m):
            copy.wait_send()
    for copy in wx_copies() + list(wy_sends()) + list(ys):
        copy.wait_send()


def finish_kernel(*refs):
    n = len(refs) // 2
    sem = refs[-1]
    copies = [pltpu.make_async_copy(refs[i], refs[n + i], sem.at[i]) for i in range(n)]
    for copy in copies:
        copy.start()
    for copy in copies:
        copy.wait()


def finish(*parts):
    far = pl.BlockSpec(memory_space=pl.ANY)
    return pl.pallas_call(
        finish_kernel,
        out_shape=tuple(jax.ShapeDtypeStruct(p.shape, p.dtype) for p in parts),
        in_specs=[pl.BlockSpec(memory_space=pltpu.VMEM)] * len(parts),
        out_specs=(far,) * len(parts),
        scratch_shapes=[pltpu.SemaphoreType.DMA((len(parts),))],
        compiler_params=pltpu.CompilerParams(vmem_limit_bytes=2**20),
        name="hand_over",
    )(*parts)


def body(tokens, expert_id, route_weight, cluster_id, out_grad, w_gate, w_up, w_down):
    vmem, far = pl.BlockSpec(memory_space=pltpu.VMEM), pl.BlockSpec(memory_space=pl.ANY)
    dma = pltpu.SemaphoreType.DMA
    rollouts = cluster_id.shape[0]
    parts = pl.pallas_call(
        kernel,
        out_shape=(
            pltpu.VMEM((TOK, FB), BF16),
            pltpu.VMEM((TOK, FB), BF16),
            pltpu.VMEM((1, FB, HID), BF16),
            pltpu.VMEM((1, FB, HID), BF16),
            pltpu.VMEM((1, HID, FB), BF16),
        ),
        in_specs=[vmem] * 3 + [far] * 5,
        out_specs=(vmem,) * 5,
        scratch_shapes=[
            pltpu.VMEM((TOK, FB), BF16),
            pltpu.VMEM((TOK, FB), BF16),
            pltpu.VMEM((ROWS, FB), BF16),
            pltpu.VMEM((ROWS, FB), BF16),
            pltpu.VMEM((4, ROWS, FB), BF16),
            pltpu.VMEM((4, ROWS, FB), BF16),
            pltpu.VMEM((4, FB, HID), BF16),
            pltpu.VMEM((4, FB, HID), BF16),
            pltpu.VMEM((4, HID, FB), BF16),
            pltpu.VMEM((3, HID, FB), BF16),
            pltpu.VMEM((ROWS, HID), F32),
            pltpu.VMEM((ROWS, HID), F32),
            pltpu.VMEM((4, ROWS, HID), BF16),
            pltpu.VMEM((4, ROWS, 2 * HID), BF16),
            pltpu.VMEM((3, ROWS, FB), BF16),
            pltpu.VMEM((CH, 2, QROWS, FB), BF16),
            pltpu.VMEM((FB, 2 * HID), F32),
            pltpu.VMEM((4, ROWS, FB), BF16),
            pltpu.VMEM((CH, 2, QROWS, FB), BF16),
            pltpu.VMEM((ROWS, FB), BF16),
            pltpu.VMEM((ROWS, FB), BF16),
            pltpu.VMEM((2, ROWS, FB), BF16),
            pltpu.VMEM((4, HID, FB), BF16),
            pltpu.VMEM((2, HID // 2, FB), BF16),
            pltpu.VMEM((HID, FB), BF16),
            pltpu.VMEM((HID, FB), BF16),
            dma((14,)),
            dma((2, NE)),
            dma((2, NE)),
            dma((2, CH, 4)),
            dma((2, CH, 4)),
            dma((CH, 6)),
            dma((CH, 6)),
            dma((2, NE)),
            dma((2, NE)),
            dma((3,)),
            dma((3,)),
            dma((4,)),
            dma((4,)),
            dma((CH, 6)),
            dma((CH, 6)),
            dma((2, 4)),
            dma((2, 4)),
            dma((2, 4)),
            dma((2, 4)),
            dma((6,)),
            dma((6,)),
        ],
        compiler_params=pltpu.CompilerParams(
            collective_id=0, has_side_effects=True, vmem_limit_bytes=LIMIT * 2**20
        ),
        name="expert_layer",
    )(
        expert_id.reshape(1, TOK),
        route_weight.reshape(1, TOK),
        cluster_id.reshape(1, rollouts),
        tokens,
        out_grad,
        w_gate,
        w_up,
        w_down,
    )
    return finish(*parts)


def solution(mesh):
    placed = (
        P(("rep", "exp"), "tp"),
        P(("rep", "exp"), None),
        P(("rep", "exp"), None),
        P(),
        P(("rep", "exp"), "tp"),
        P("exp", None, "tp"),
        P("exp", None, "tp"),
        P("exp", "tp", None),
    )
    return jax.shard_map(
        body,
        mesh=mesh,
        in_specs=placed,
        out_specs=(
            P(("rep", "exp"), "tp"),
            P(("rep", "exp"), "tp"),
            P("exp", "rep", "tp"),
            P("exp", "rep", "tp"),
            P("exp", "tp", "rep"),
        ),
        check_vma=False,
    )
```

```python
import jax
import jax.numpy as jnp
from jax import lax
from jax.experimental import pallas as pl
from jax.experimental.pallas import tpu as pltpu
from jax.sharding import PartitionSpec as P

MESH = pl.DeviceIdType.MESH
F32, BF16 = jnp.float32, jnp.bfloat16
TOK = 128
CAP = 32
NE = 16
ROWS = NE * CAP
FB = 1024
HID = 384
GROUP = 16
LIMIT = 56
CH = 4
CROWS = ROWS // CH
HROWS = ROWS // 2
QROWS = CROWS // 2
FAR = (0, 1, 3, 5, 4, 7, 2, 6)


def dot_nn(a, b):
    return lax.dot_general(a, b, (((1,), (0,)), ((), ())), preferred_element_type=F32)


def dot_nt(a, b):
    return lax.dot_general(a, b, (((1,), (1,)), ((), ())), preferred_element_type=F32)


def dot_tn(a, b):
    return lax.dot_general(a, b, (((0,), (0,)), ((), ())), preferred_element_type=F32)


def kernel(
    eid_row,
    weight_row,
    clu_row,
    tokens_far,
    out_grad_far,
    w_gate,
    w_up,
    w_down,
    mixed,
    grad_tokens,
    out_gate,
    out_up,
    out_down,
    tokens,
    out_grad,
    send_t,
    send_c,
    rows_t,
    rows_c,
    wg,
    wu,
    wd,
    wdx,
    slope,
    silu,
    hid,
    gpy,
    rows_y,
    relay,
    acc,
    part_i,
    x_one,
    x_left,
    x_right,
    ret,
    g_dn,
    y_one,
    y_left,
    y_right,
    w_sem,
    z_ssem,
    z_rsem,
    ag_ssem,
    ag_rsem,
    rs_ssem,
    rs_rsem,
    zr_ssem,
    zr_rsem,
    wx_ssem,
    wx_rsem,
    wy_ssem,
    wy_rsem,
    ty_ssem,
    ty_rsem,
    hd_ssem,
    hd_rsem,
    gp_ssem,
    gp_rsem,
    y_ssem,
    y_rsem,
):
    x, y, e = lax.axis_index("tp"), lax.axis_index("rep"), lax.axis_index("exp")
    z, core = e // 2, e % 2
    x_next, x_prev = {"tp": (x + 1) % 4}, {"tp": (x + 3) % 4}
    y_next, y_prev = {"rep": (y + 1) % 4}, {"rep": (y + 3) % 4}
    x_far = {"tp": (x + 2) % 4}

    def to_of(j):
        return {"exp": ((z + FAR[j // 2]) % 8) * 2 + (core + j % 2) % 2}

    def from_of(j):
        return {"exp": ((z + 8 - FAR[j // 2]) % 8) * 2 + (core + j % 2) % 2}

    def remote(src, dst, ssem, rsem, where):
        return pltpu.make_async_remote_copy(
            src_ref=src,
            dst_ref=dst,
            send_sem=ssem,
            recv_sem=rsem,
            device_id=where,
            device_id_type=MESH,
        )

    barrier = pltpu.get_barrier_semaphore()
    for where in [to_of(j) for j in range(1, NE)] + [x_next, x_prev, x_far, y_next, y_prev]:
        pl.semaphore_signal(barrier, inc=1, device_id=where, device_id_type=MESH)
    load_t = pltpu.make_async_copy(tokens_far, tokens, w_sem.at[12])
    load_t.start()
    load_c = pltpu.make_async_copy(out_grad_far, out_grad, w_sem.at[13])
    load_c.start()

    loads, loads_d = [], []
    for i in range(4):
        at = pl.ds(pl.multiple_of(((x + i) % 4) * FB, FB), FB)
        loads.append(pltpu.make_async_copy(w_gate.at[0, at, :], wg.at[i], w_sem.at[i]))
        loads.append(pltpu.make_async_copy(w_up.at[0, at, :], wu.at[i], w_sem.at[4 + i]))
        loads_d.append(pltpu.make_async_copy(w_down.at[0, :, at], wd.at[i], w_sem.at[8 + i]))
    for load in loads_d + loads:
        load.start()

    def place(ids):
        away = ((ids >> 1) - z + 8) & 7
        first = sum(jnp.where(away == far, n, 0) for n, far in enumerate(FAR))
        return (2 * first + (((ids & 1) + core) & 1)) * CAP

    sub = lax.broadcasted_iota(jnp.int32, (TOK, TOK), 0)
    lane = lax.broadcasted_iota(jnp.int32, (TOK, TOK), 1)

    def column(row):
        return jnp.sum(jnp.where(sub == lane, row, 0), axis=1, keepdims=True)

    ids_row = eid_row[...]
    ids_col = column(ids_row)
    same = ids_col == ids_row
    rank_col = jnp.sum(jnp.where(same & (lane < sub), 1.0, 0.0), axis=1, keepdims=True)
    rank_row = jnp.sum(jnp.where(same & (sub < lane), 1.0, 0.0), axis=0, keepdims=True)
    slot_col = place(ids_col) + rank_col.astype(jnp.int32)
    slot_row = place(ids_row) + rank_row.astype(jnp.int32)
    pick = jnp.where(
        lax.broadcasted_iota(jnp.int32, (ROWS, TOK), 0) == slot_row, 1.0, 0.0
    ).astype(BF16)
    load_t.wait()
    send_t[...] = dot_nn(pick, tokens[...]).astype(BF16)

    pl.semaphore_wait(barrier, NE - 1 + 5)

    def z_copy(k, j):
        src, dst = ((send_t, rows_t), (send_c, rows_c))[k]
        at = pl.ds(j * CAP, CAP)
        return remote(src.at[at], dst.at[0, at], z_ssem.at[k, j], z_rsem.at[k, j], to_of(j))

    def z_start(k, c):
        for j in range(max(4 * c, 1), 4 * c + 4):
            z_copy(k, j).start()

    z_start(0, 0)
    z_start(0, 1)
    rows_t[0, 0:CAP, :] = send_t[0:CAP, :]

    weight = column(weight_row[...])

    def make_cotangent():
        same_group = (sub // GROUP) == (lane // GROUP)
        votes = jnp.where((column(clu_row[...]) == clu_row[...]) & same_group, 1.0, 0.0)
        agree_row = jnp.sum(votes, axis=0, keepdims=True)
        agree_col = jnp.sum(votes, axis=1, keepdims=True)
        mean_row = jnp.sum(jnp.where(same_group, agree_col, 0.0), axis=0, keepdims=True) * (1.0 / GROUP)
        own = 2 * (y * NE + e) + sub // (TOK // 2)
        adv = jnp.sum(jnp.where(lane == own, agree_row - mean_row, 0.0), axis=1, keepdims=True)
        load_c.wait()
        cot = ((adv * weight) * out_grad[...].astype(F32)).astype(BF16)
        send_c[...] = dot_nn(pick, cot).astype(BF16)
        rows_c[0, 0:CAP, :] = send_c[0:CAP, :]

    def ring(buf, first, count, ssem, rsem, where, nxt, prv):
        lo = pl.ds(first, count)
        a, b = pl.ds(first, count // 2), pl.ds(first + count // 2, count // 2)
        s, r = [ssem.at[*where, n] for n in range(4)], [rsem.at[*where, n] for n in range(4)]
        return (
            remote(buf.at[0, lo], buf.at[3, lo], s[0], r[0], nxt),
            remote(buf.at[0, lo], buf.at[1, lo], s[1], r[1], prv),
            remote(buf.at[3, a], buf.at[2, a], s[2], r[2], nxt),
            remote(buf.at[1, b], buf.at[2, b], s[3], r[3], prv),
        )

    def ag_copies(k, c):
        buf = (rows_t, rows_c)[k]
        return ring(buf, c * CROWS, CROWS, ag_ssem, ag_rsem, (k, c), x_next, x_prev)

    def hd_copies(m):
        return ring(hid, m * HROWS, HROWS, hd_ssem, hd_rsem, (m,), x_next, x_prev)

    def gp_copies(m):
        return ring(gpy, m * HROWS, HROWS, gp_ssem, gp_rsem, (m,), y_next, y_prev)

    def begin(copies):
        for copy in copies[:2]:
            copy.start()

    def forward(copies):
        copies[0].wait_recv()
        copies[2].start()
        copies[1].wait_recv()
        copies[3].start()

    def ag_send(k, c):
        for j in range(max(4 * c, 1), 4 * c + 4):
            z_copy(k, j).wait_recv()
        for copy in ag_copies(k, c)[:2]:
            copy.start()

    def ag_forward(k, c):
        forward(ag_copies(k, c))

    def ag_wait(k, c):
        for copy in ag_copies(k, c)[2:]:
            copy.wait_recv()

    def hrows(m):
        return pl.ds(m * HROWS, HROWS)

    def first_layer(m):
        at = hrows(m)
        pre_g = dot_nn(rows_t[0, at, :], wg[0])
        for i in range(1, 4):
            pre_g += dot_nn(rows_t[i, at, :], wg[i])
        slope[at, :] = pre_g
        pre_u = dot_nn(rows_t[0, at, :], wu[0])
        for i in range(1, 4):
            pre_u += dot_nn(rows_t[i, at, :], wu[i])
        pre_g = slope[at, :]
        sig = jax.nn.sigmoid(pre_g)
        act = pre_g * sig
        hid[0, at, :] = (act * pre_u).astype(BF16)
        silu[at, :] = act
        slope[at, :] = pre_u * sig * (1.0 + pre_g * (1.0 - sig))

    QD = HID // 4

    def quarter(k, half=None):
        first = ((y + k) % 4) * QD
        if half is None:
            return pl.ds(pl.multiple_of(first, QD), QD)
        return pl.ds(pl.multiple_of(first + half * (QD // 2), QD // 2), QD // 2)

    def wx_copies():
        return [
            remote(
                wd.at[i, quarter(0)], wdx.at[3 - i, quarter(0)], wx_ssem.at[i - 1], wx_rsem.at[i - 1], where
            )
            for i, where in ((1, x_next), (2, x_far), (3, x_prev))
        ]

    def wy_copy(n, at, where):
        return remote(wdx.at[:, at], wdx.at[:, at], wy_ssem.at[n], wy_rsem.at[n], where)

    def wy_sends():
        return (
            wy_copy(0, quarter(0), y_next),
            wy_copy(1, quarter(0), y_prev),
            wy_copy(2, quarter(3, 0), y_next),
            wy_copy(3, quarter(1, 1), y_prev),
        )

    def wy_recvs():
        return (
            wy_copy(0, quarter(3), y_next),
            wy_copy(1, quarter(1), y_prev),
            wy_copy(2, quarter(2, 0), y_next),
            wy_copy(3, quarter(2, 1), y_prev),
        )

    def block(k):
        return (y + k - x + 4) % 4

    def ty_copies(m):
        lo = pl.ds(m * CROWS, CROWS)
        a, b = pl.ds(m * CROWS, QROWS), pl.ds(m * CROWS + QROWS, QROWS)
        s, r = ty_ssem, ty_rsem
        return (
            remote(rows_t.at[block(2), a], relay.at[m, 0], s.at[m, 0], r.at[m, 0], y_next),
            remote(rows_t.at[block(2), b], relay.at[m, 1], s.at[m, 1], r.at[m, 1], y_prev),
            remote(rows_t.at[block(1), lo], rows_y.at[2, lo], s.at[m, 2], r.at[m, 2], y_next),
            remote(rows_t.at[block(3), lo], rows_y.at[0, lo], s.at[m, 3], r.at[m, 3], y_prev),
            remote(relay.at[m, 0], rows_y.at[1, a], s.at[m, 4], r.at[m, 4], y_next),
            remote(relay.at[m, 1], rows_y.at[1, b], s.at[m, 5], r.at[m, 5], y_prev),
        )

    def ty_first(m):
        ag_wait(0, m)
        for copy in ty_copies(m)[:4]:
            copy.start()

    def ty_forward(m):
        copies = ty_copies(m)
        for n in range(2):
            copies[n].wait_recv()
            copies[4 + n].start()

    def back_hidden(first, count):
        at = pl.ds(first, count)
        grad = dot_nt(rows_c[0, at, :], wd[0])
        for i in range(1, 4):
            grad += dot_nt(rows_c[i, at, :], wd[i])
        gpy[0, at, 0:HID] = (grad * slope[at, :]).astype(BF16)
        gpy[0, at, HID:] = (grad * silu[at, :]).astype(BF16)

    def back_tokens(first, count):
        at = pl.ds(first, count)

        @pl.loop(0, 4)
        def _(i):
            part_i[i, at, :] = (
                dot_nt(gpy[0, at, 0:HID], wg[i]) + dot_nt(gpy[0, at, HID:], wu[i])
            ).astype(BF16)

    ORDER = (2, 1, 3, 0)

    def down_grads(k):
        i = block(ORDER[k])

        @pl.loop(0, 4)
        def _(f):
            at = pl.ds(pl.multiple_of(f * 256, 256), 256)
            g_dn[k, :, at] = dot_tn(hid[0], rows_c[i, :, at]).astype(BF16)

    def gate_up_grads(k, last=False):
        rows = rows_t.at[block(0)] if k == 0 else rows_y.at[k - 1]

        @pl.loop(0, 4)
        def _(f):
            at = pl.ds(pl.multiple_of(f * 256, 256), 256)
            term = dot_tn(rows[:, at], gpy[k])
            if k == 0:
                acc[at, :] = term
            elif not last:
                acc[at, :] += term
            else:
                both = (acc[at, :] + term).astype(BF16)
                out_gate[0, at, :] = both[:, :HID]
                out_up[0, at, :] = both[:, HID:]

    def rs_copies(m):
        a, b = pl.ds(m * CROWS, QROWS), pl.ds(m * CROWS + QROWS, QROWS)
        s, r = rs_ssem, rs_rsem
        return (
            remote(part_i.at[2, a], x_one.at[m, 0], s.at[m, 0], r.at[m, 0], x_next),
            remote(part_i.at[2, b], x_one.at[m, 1], s.at[m, 1], r.at[m, 1], x_prev),
            remote(part_i.at[1, b], x_left.at[b], s.at[m, 2], r.at[m, 2], x_next),
            remote(part_i.at[3, a], x_right.at[a], s.at[m, 3], r.at[m, 3], x_prev),
            remote(part_i.at[1, a], x_left.at[a], s.at[m, 4], r.at[m, 4], x_next),
            remote(part_i.at[3, b], x_right.at[b], s.at[m, 5], r.at[m, 5], x_prev),
        )

    def add_into(ref, at, other):
        ref[at] = (ref[at].astype(F32) + other.astype(F32)).astype(BF16)

    def rs_first(m):
        for copy in rs_copies(m)[:4]:
            copy.start()

    def rs_pass_on(m):
        copies = rs_copies(m)
        copies[0].wait_recv()
        add_into(part_i, (1, pl.ds(m * CROWS, QROWS)), x_one[m, 0])
        copies[4].start()
        copies[1].wait_recv()
        add_into(part_i, (3, pl.ds(m * CROWS + QROWS, QROWS)), x_one[m, 1])
        copies[5].start()

    total = (send_t, send_c)

    def zr_copy(k, j):
        at = pl.ds(j * CAP, CAP)
        return remote(
            total[k].at[at], ret.at[k, at], zr_ssem.at[k, j], zr_rsem.at[k, j], from_of(j)
        )

    def zr_start(k, m):
        for j in range(max(m * 4, 1), m * 4 + 4):
            zr_copy(k, j).start()
        if m == 0:
            ret[k, 0:CAP, :] = total[k][0:CAP, :]

    def rs_last(m):
        for copy in rs_copies(m)[2:]:
            copy.wait_recv()
        at = pl.ds(m * CROWS, CROWS)
        total[1][at, :] = (
            part_i[0, at, :].astype(F32) + x_left[at, :].astype(F32) + x_right[at, :].astype(F32)
        ).astype(BF16)
        zr_start(1, m)

    def second_layer(m):
        for copy in hd_copies(m)[2:]:
            copy.wait_recv()
        at = hrows(m)
        out = dot_nn(hid[0, at, :], wd[0])
        for i in range(1, 4):
            out += dot_nn(hid[i, at, :], wdx[i - 1])
        total[0][at, :] = out.astype(BF16)
        zr_start(0, 2 * m + 1)
        zr_start(0, 2 * m)

    def back(k):
        for j in range(1, NE):
            zr_copy(k, j).wait_recv()
        spread = jnp.where(
            lax.broadcasted_iota(jnp.int32, (TOK, ROWS), 1) == slot_col, 1.0, 0.0
        ).astype(BF16)
        return dot_nn(spread, ret[k])

    HH = HID // 2
    dn_a, dn_b = pl.ds(0, HH), pl.ds(HH, HH)

    def y_copies():
        s, r = y_ssem, y_rsem
        return (
            remote(g_dn.at[0, dn_a], y_one.at[0], s.at[0], r.at[0], y_next),
            remote(g_dn.at[0, dn_b], y_one.at[1], s.at[1], r.at[1], y_prev),
            remote(g_dn.at[1, dn_b], y_left.at[dn_b], s.at[2], r.at[2], y_next),
            remote(g_dn.at[2, dn_a], y_right.at[dn_a], s.at[3], r.at[3], y_prev),
            remote(g_dn.at[1, dn_a], y_left.at[dn_a], s.at[4], r.at[4], y_next),
            remote(g_dn.at[2, dn_b], y_right.at[dn_b], s.at[5], r.at[5], y_prev),
        )

    for load in loads_d:
        load.wait()
    for copy in wx_copies():
        copy.start()
    ag_send(0, 0)
    z_start(0, 2)
    make_cotangent()
    ag_send(0, 1)
    z_start(0, 3)
    for copy in wx_copies():
        copy.wait_recv()
    begin(wy_sends())
    ag_forward(0, 0)
    ag_send(0, 2)
    z_start(1, 0)
    z_start(1, 1)
    ag_forward(0, 1)
    ty_first(0)
    ag_send(0, 3)
    z_start(1, 2)
    ag_forward(0, 2)
    ty_first(1)
    z_start(1, 3)
    ag_send(1, 0)
    ag_forward(0, 3)
    for n in range(2):
        wy_recvs()[n].wait_recv()
        wy_sends()[2 + n].start()
    ty_first(2)
    ty_forward(0)
    ag_send(1, 1)
    for load in loads:
        load.wait()
    first_layer(0)
    begin(hd_copies(0))
    ag_send(1, 2)
    ag_forward(1, 0)
    ag_send(1, 3)
    ty_first(3)
    ty_forward(1)
    first_layer(1)
    ag_forward(1, 1)
    ty_forward(2)
    forward(hd_copies(0))
    ag_forward(1, 2)
    ag_wait(1, 0)
    ag_wait(1, 1)
    back_hidden(0, HROWS)
    begin(gp_copies(0))
    for k in range(2):
        for j in range(1, NE):
            z_copy(k, j).wait_send()
    for copy in wy_recvs()[2:]:
        copy.wait_recv()
    second_layer(0)
    back_tokens(0, HROWS)
    ty_forward(3)
    ag_forward(1, 3)
    begin(hd_copies(1))
    rs_first(1)
    ag_wait(1, 2)
    back_hidden(2 * CROWS, CROWS)
    ag_wait(1, 3)
    back_hidden(3 * CROWS, CROWS)
    begin(gp_copies(1))
    ys = y_copies()
    down_grads(0)
    ys[0].start()
    ys[1].start()
    forward(hd_copies(1))
    back_tokens(3 * CROWS, CROWS)
    rs_first(3)
    rs_pass_on(1)
    back_tokens(2 * CROWS, CROWS)
    rs_first(2)
    second_layer(1)
    forward(gp_copies(0))
    down_grads(1)
    ys[2].start()
    down_grads(2)
    ys[3].start()
    rs_pass_on(3)
    rs_first(0)
    rs_pass_on(2)
    rs_last(1)
    gate_up_grads(0)
    forward(gp_copies(1))
    rs_last(3)
    ys[0].wait_recv()
    add_into(g_dn, (1, dn_a), y_one[0])
    ys[4].start()
    ys[1].wait_recv()
    add_into(g_dn, (2, dn_b), y_one[1])
    ys[5].start()
    rs_pass_on(0)
    for m in range(CH):
        ty_copies(m)[2].wait_recv()
        ty_copies(m)[3].wait_recv()
    gate_up_grads(3)
    rs_last(2)
    gate_up_grads(1)
    rs_last(0)
    down_grads(3)
    mixed[...] = (weight * back(0).astype(BF16).astype(F32)).astype(BF16)
    for m in range(CH):
        ty_copies(m)[4].wait_recv()
        ty_copies(m)[5].wait_recv()
    for m in range(2):
        gp_copies(m)[2].wait_recv()
        gp_copies(m)[3].wait_recv()
    gate_up_grads(2, last=True)
    for copy in ys[2:]:
        copy.wait_recv()
    out_down[0] = (
        g_dn[3].astype(F32) + y_left[...].astype(F32) + y_right[...].astype(F32)
    ).astype(BF16)
    grad_tokens[...] = back(1).astype(BF16)

    for k in range(2):
        for c in range(CH):
            for copy in ag_copies(k, c):
                copy.wait_send()
        for copy in hd_copies(k) + gp_copies(k):
            copy.wait_send()
        for j in range(1, NE):
            zr_copy(k, j).wait_send()
    for m in range(CH):
        for copy in ty_copies(m) + rs_copies(m):
            copy.wait_send()
    for copy in wx_copies() + list(wy_sends()) + list(ys):
        copy.wait_send()


def finish_kernel(*refs):
    n = len(refs) // 2
    sem = refs[-1]
    copies = [pltpu.make_async_copy(refs[i], refs[n + i], sem.at[i]) for i in range(n)]
    for copy in copies:
        copy.start()
    for copy in copies:
        copy.wait()


def finish(*parts):
    far = pl.BlockSpec(memory_space=pl.ANY)
    return pl.pallas_call(
        finish_kernel,
        out_shape=tuple(jax.ShapeDtypeStruct(p.shape, p.dtype) for p in parts),
        in_specs=[pl.BlockSpec(memory_space=pltpu.VMEM)] * len(parts),
        out_specs=(far,) * len(parts),
        scratch_shapes=[pltpu.SemaphoreType.DMA((len(parts),))],
        compiler_params=pltpu.CompilerParams(vmem_limit_bytes=2**20),
        name="hand_over",
    )(*parts)


def body(tokens, expert_id, route_weight, cluster_id, out_grad, w_gate, w_up, w_down):
    vmem, far = pl.BlockSpec(memory_space=pltpu.VMEM), pl.BlockSpec(memory_space=pl.ANY)
    dma = pltpu.SemaphoreType.DMA
    rollouts = cluster_id.shape[0]
    parts = pl.pallas_call(
        kernel,
        out_shape=(
            pltpu.VMEM((TOK, FB), BF16),
            pltpu.VMEM((TOK, FB), BF16),
            pltpu.VMEM((1, FB, HID), BF16),
            pltpu.VMEM((1, FB, HID), BF16),
            pltpu.VMEM((1, HID, FB), BF16),
        ),
        in_specs=[vmem] * 3 + [far] * 5,
        out_specs=(vmem,) * 5,
        scratch_shapes=[
            pltpu.VMEM((TOK, FB), BF16),
            pltpu.VMEM((TOK, FB), BF16),
            pltpu.VMEM((ROWS, FB), BF16),
            pltpu.VMEM((ROWS, FB), BF16),
            pltpu.VMEM((4, ROWS, FB), BF16),
            pltpu.VMEM((4, ROWS, FB), BF16),
            pltpu.VMEM((4, FB, HID), BF16),
            pltpu.VMEM((4, FB, HID), BF16),
            pltpu.VMEM((4, HID, FB), BF16),
            pltpu.VMEM((3, HID, FB), BF16),
            pltpu.VMEM((ROWS, HID), F32),
            pltpu.VMEM((ROWS, HID), F32),
            pltpu.VMEM((4, ROWS, HID), BF16),
            pltpu.VMEM((4, ROWS, 2 * HID), BF16),
            pltpu.VMEM((3, ROWS, FB), BF16),
            pltpu.VMEM((CH, 2, QROWS, FB), BF16),
            pltpu.VMEM((FB, 2 * HID), F32),
            pltpu.VMEM((4, ROWS, FB), BF16),
            pltpu.VMEM((CH, 2, QROWS, FB), BF16),
            pltpu.VMEM((ROWS, FB), BF16),
            pltpu.VMEM((ROWS, FB), BF16),
            pltpu.VMEM((2, ROWS, FB), BF16),
            pltpu.VMEM((4, HID, FB), BF16),
            pltpu.VMEM((2, HID // 2, FB), BF16),
            pltpu.VMEM((HID, FB), BF16),
            pltpu.VMEM((HID, FB), BF16),
            dma((14,)),
            dma((2, NE)),
            dma((2, NE)),
            dma((2, CH, 4)),
            dma((2, CH, 4)),
            dma((CH, 6)),
            dma((CH, 6)),
            dma((2, NE)),
            dma((2, NE)),
            dma((3,)),
            dma((3,)),
            dma((4,)),
            dma((4,)),
            dma((CH, 6)),
            dma((CH, 6)),
            dma((2, 4)),
            dma((2, 4)),
            dma((2, 4)),
            dma((2, 4)),
            dma((6,)),
            dma((6,)),
        ],
        compiler_params=pltpu.CompilerParams(
            collective_id=0, has_side_effects=True, vmem_limit_bytes=LIMIT * 2**20
        ),
        name="expert_layer",
    )(
        expert_id.reshape(1, TOK),
        route_weight.reshape(1, TOK),
        cluster_id.reshape(1, rollouts),
        tokens,
        out_grad,
        w_gate,
        w_up,
        w_down,
    )
    return finish(*parts)


def solution(mesh):
    placed = (
        P(("rep", "exp"), "tp"),
        P(("rep", "exp"), None),
        P(("rep", "exp"), None),
        P(),
        P(("rep", "exp"), "tp"),
        P("exp", None, "tp"),
        P("exp", None, "tp"),
        P("exp", "tp", None),
    )
    return jax.shard_map(
        body,
        mesh=mesh,
        in_specs=placed,
        out_specs=(
            P(("rep", "exp"), "tp"),
            P(("rep", "exp"), "tp"),
            P("exp", "rep", "tp"),
            P("exp", "rep", "tp"),
            P("exp", "tp", "rep"),
        ),
        check_vma=False,
    )
```

```python
import jax
import jax.numpy as jnp
from jax import lax
from jax.experimental import pallas as pl
from jax.experimental.pallas import tpu as pltpu
from jax.sharding import PartitionSpec as P

MESH = pl.DeviceIdType.MESH
F32, BF16 = jnp.float32, jnp.bfloat16
TOK = 128
CAP = 32
NE = 16
ROWS = NE * CAP
FB = 1024
HID = 384
GROUP = 16
LIMIT = 56
CH = 4
CROWS = ROWS // CH
HROWS = ROWS // 2
QROWS = CROWS // 2
FAR = (0, 1, 3, 5, 4, 7, 2, 6)


def dot_nn(a, b):
    return lax.dot_general(a, b, (((1,), (0,)), ((), ())), preferred_element_type=F32)


def dot_nt(a, b):
    return lax.dot_general(a, b, (((1,), (1,)), ((), ())), preferred_element_type=F32)


def dot_tn(a, b):
    return lax.dot_general(a, b, (((0,), (0,)), ((), ())), preferred_element_type=F32)


def kernel(
    eid_row,
    weight_row,
    clu_row,
    tokens_far,
    out_grad_far,
    w_gate,
    w_up,
    w_down,
    mixed,
    grad_tokens,
    out_gate,
    out_up,
    out_down,
    tokens,
    out_grad,
    send_t,
    send_c,
    rows_t,
    rows_c,
    wg,
    wu,
    wd,
    wdx,
    slope,
    silu,
    hid,
    gpy,
    rows_y,
    relay,
    acc,
    part_i,
    x_one,
    x_left,
    x_right,
    ret,
    g_dn,
    y_one,
    y_left,
    y_right,
    w_sem,
    z_ssem,
    z_rsem,
    ag_ssem,
    ag_rsem,
    rs_ssem,
    rs_rsem,
    zr_ssem,
    zr_rsem,
    wx_ssem,
    wx_rsem,
    wy_ssem,
    wy_rsem,
    ty_ssem,
    ty_rsem,
    hd_ssem,
    hd_rsem,
    gp_ssem,
    gp_rsem,
    y_ssem,
    y_rsem,
):
    x, y, e = lax.axis_index("tp"), lax.axis_index("rep"), lax.axis_index("exp")
    z, core = e // 2, e % 2
    x_next, x_prev = {"tp": (x + 1) % 4}, {"tp": (x + 3) % 4}
    y_next, y_prev = {"rep": (y + 1) % 4}, {"rep": (y + 3) % 4}
    x_far = {"tp": (x + 2) % 4}

    def to_of(j):
        return {"exp": ((z + FAR[j // 2]) % 8) * 2 + (core + j % 2) % 2}

    def from_of(j):
        return {"exp": ((z + 8 - FAR[j // 2]) % 8) * 2 + (core + j % 2) % 2}

    def remote(src, dst, ssem, rsem, where):
        return pltpu.make_async_remote_copy(
            src_ref=src,
            dst_ref=dst,
            send_sem=ssem,
            recv_sem=rsem,
            device_id=where,
            device_id_type=MESH,
        )

    barrier = pltpu.get_barrier_semaphore()
    for where in [to_of(j) for j in range(1, NE)] + [x_next, x_prev, x_far, y_next, y_prev]:
        pl.semaphore_signal(barrier, inc=1, device_id=where, device_id_type=MESH)
    load_t = pltpu.make_async_copy(tokens_far, tokens, w_sem.at[12])
    load_t.start()
    load_c = pltpu.make_async_copy(out_grad_far, out_grad, w_sem.at[13])
    load_c.start()

    loads, loads_d = [], []
    for i in range(4):
        at = pl.ds(pl.multiple_of(((x + i) % 4) * FB, FB), FB)
        loads.append(pltpu.make_async_copy(w_gate.at[0, at, :], wg.at[i], w_sem.at[i]))
        loads.append(pltpu.make_async_copy(w_up.at[0, at, :], wu.at[i], w_sem.at[4 + i]))
        loads_d.append(pltpu.make_async_copy(w_down.at[0, :, at], wd.at[i], w_sem.at[8 + i]))
    for load in loads_d + loads:
        load.start()

    def place(ids):
        away = ((ids >> 1) - z + 8) & 7
        first = sum(jnp.where(away == far, n, 0) for n, far in enumerate(FAR))
        return (2 * first + (((ids & 1) + core) & 1)) * CAP

    sub = lax.broadcasted_iota(jnp.int32, (TOK, TOK), 0)
    lane = lax.broadcasted_iota(jnp.int32, (TOK, TOK), 1)

    def column(row):
        return jnp.sum(jnp.where(sub == lane, row, 0), axis=1, keepdims=True)

    ids_row = eid_row[...]
    ids_col = column(ids_row)
    same = ids_col == ids_row
    rank_col = jnp.sum(jnp.where(same & (lane < sub), 1.0, 0.0), axis=1, keepdims=True)
    rank_row = jnp.sum(jnp.where(same & (sub < lane), 1.0, 0.0), axis=0, keepdims=True)
    slot_col = place(ids_col) + rank_col.astype(jnp.int32)
    slot_row = place(ids_row) + rank_row.astype(jnp.int32)
    pick = jnp.where(
        lax.broadcasted_iota(jnp.int32, (ROWS, TOK), 0) == slot_row, 1.0, 0.0
    ).astype(BF16)
    load_t.wait()
    send_t[0:CROWS, :] = dot_nn(pick[0:CROWS], tokens[...]).astype(BF16)

    pl.semaphore_wait(barrier, NE - 1 + 5)

    def z_copy(k, j):
        src, dst = ((send_t, rows_t), (send_c, rows_c))[k]
        at = pl.ds(j * CAP, CAP)
        return remote(src.at[at], dst.at[0, at], z_ssem.at[k, j], z_rsem.at[k, j], to_of(j))

    def z_start(k, c):
        for j in range(max(4 * c, 1), 4 * c + 4):
            z_copy(k, j).start()

    z_start(0, 0)
    send_t[CROWS:, :] = dot_nn(pick[CROWS:], tokens[...]).astype(BF16)
    z_start(0, 1)
    rows_t[0, 0:CAP, :] = send_t[0:CAP, :]

    weight = column(weight_row[...])

    def make_cotangent():
        same_group = (sub // GROUP) == (lane // GROUP)
        votes = jnp.where((column(clu_row[...]) == clu_row[...]) & same_group, 1.0, 0.0)
        agree_row = jnp.sum(votes, axis=0, keepdims=True)
        agree_col = jnp.sum(votes, axis=1, keepdims=True)
        mean_row = jnp.sum(jnp.where(same_group, agree_col, 0.0), axis=0, keepdims=True) * (1.0 / GROUP)
        own = 2 * (y * NE + e) + sub // (TOK // 2)
        adv = jnp.sum(jnp.where(lane == own, agree_row - mean_row, 0.0), axis=1, keepdims=True)
        load_c.wait()
        cot = ((adv * weight) * out_grad[...].astype(F32)).astype(BF16)
        send_c[...] = dot_nn(pick, cot).astype(BF16)
        rows_c[0, 0:CAP, :] = send_c[0:CAP, :]

    def ring(buf, first, count, ssem, rsem, where, nxt, prv):
        lo = pl.ds(first, count)
        a, b = pl.ds(first, count // 2), pl.ds(first + count // 2, count // 2)
        s, r = [ssem.at[*where, n] for n in range(4)], [rsem.at[*where, n] for n in range(4)]
        return (
            remote(buf.at[0, lo], buf.at[3, lo], s[0], r[0], nxt),
            remote(buf.at[0, lo], buf.at[1, lo], s[1], r[1], prv),
            remote(buf.at[3, a], buf.at[2, a], s[2], r[2], nxt),
            remote(buf.at[1, b], buf.at[2, b], s[3], r[3], prv),
        )

    def ag_copies(k, c):
        buf = (rows_t, rows_c)[k]
        return ring(buf, c * CROWS, CROWS, ag_ssem, ag_rsem, (k, c), x_next, x_prev)

    def hd_copies(m):
        return ring(hid, m * HROWS, HROWS, hd_ssem, hd_rsem, (m,), x_next, x_prev)

    def gp_copies(m):
        return ring(gpy, m * HROWS, HROWS, gp_ssem, gp_rsem, (m,), y_next, y_prev)

    def begin(copies):
        for copy in copies[:2]:
            copy.start()

    def forward(copies):
        copies[0].wait_recv()
        copies[2].start()
        copies[1].wait_recv()
        copies[3].start()

    def ag_send(k, c):
        for j in range(max(4 * c, 1), 4 * c + 4):
            z_copy(k, j).wait_recv()
        for copy in ag_copies(k, c)[:2]:
            copy.start()

    def ag_forward(k, c):
        forward(ag_copies(k, c))

    def ag_wait(k, c):
        for copy in ag_copies(k, c)[2:]:
            copy.wait_recv()

    def hrows(m):
        return pl.ds(m * HROWS, HROWS)

    def first_layer(m):
        at = hrows(m)
        pre_g = dot_nn(rows_t[0, at, :], wg[0])
        for i in range(1, 4):
            pre_g += dot_nn(rows_t[i, at, :], wg[i])
        slope[at, :] = pre_g
        pre_u = dot_nn(rows_t[0, at, :], wu[0])
        for i in range(1, 4):
            pre_u += dot_nn(rows_t[i, at, :], wu[i])
        pre_g = slope[at, :]
        sig = jax.nn.sigmoid(pre_g)
        act = pre_g * sig
        hid[0, at, :] = (act * pre_u).astype(BF16)
        silu[at, :] = act
        slope[at, :] = pre_u * sig * (1.0 + pre_g * (1.0 - sig))

    QD = HID // 4

    def quarter(k, half=None):
        first = ((y + k) % 4) * QD
        if half is None:
            return pl.ds(pl.multiple_of(first, QD), QD)
        return pl.ds(pl.multiple_of(first + half * (QD // 2), QD // 2), QD // 2)

    def wx_copies():
        return [
            remote(
                wd.at[i, quarter(0)], wdx.at[3 - i, quarter(0)], wx_ssem.at[i - 1], wx_rsem.at[i - 1], where
            )
            for i, where in ((1, x_next), (2, x_far), (3, x_prev))
        ]

    def wy_copy(n, at, where):
        return remote(wdx.at[:, at], wdx.at[:, at], wy_ssem.at[n], wy_rsem.at[n], where)

    def wy_sends():
        return (
            wy_copy(0, quarter(0), y_next),
            wy_copy(1, quarter(0), y_prev),
            wy_copy(2, quarter(3, 0), y_next),
            wy_copy(3, quarter(1, 1), y_prev),
        )

    def wy_recvs():
        return (
            wy_copy(0, quarter(3), y_next),
            wy_copy(1, quarter(1), y_prev),
            wy_copy(2, quarter(2, 0), y_next),
            wy_copy(3, quarter(2, 1), y_prev),
        )

    def block(k):
        return (y + k - x + 4) % 4

    def ty_copies(m):
        lo = pl.ds(m * CROWS, CROWS)
        a, b = pl.ds(m * CROWS, QROWS), pl.ds(m * CROWS + QROWS, QROWS)
        s, r = ty_ssem, ty_rsem
        return (
            remote(rows_t.at[block(2), a], relay.at[m, 0], s.at[m, 0], r.at[m, 0], y_next),
            remote(rows_t.at[block(2), b], relay.at[m, 1], s.at[m, 1], r.at[m, 1], y_prev),
            remote(rows_t.at[block(1), lo], rows_y.at[2, lo], s.at[m, 2], r.at[m, 2], y_next),
            remote(rows_t.at[block(3), lo], rows_y.at[0, lo], s.at[m, 3], r.at[m, 3], y_prev),
            remote(relay.at[m, 0], rows_y.at[1, a], s.at[m, 4], r.at[m, 4], y_next),
            remote(relay.at[m, 1], rows_y.at[1, b], s.at[m, 5], r.at[m, 5], y_prev),
        )

    def ty_first(m):
        ag_wait(0, m)
        for copy in ty_copies(m)[:4]:
            copy.start()

    def ty_forward(m):
        copies = ty_copies(m)
        for n in range(2):
            copies[n].wait_recv()
            copies[4 + n].start()

    def back_hidden(first, count):
        at = pl.ds(first, count)
        grad = dot_nt(rows_c[0, at, :], wd[0])
        for i in range(1, 4):
            grad += dot_nt(rows_c[i, at, :], wd[i])
        gpy[0, at, 0:HID] = (grad * slope[at, :]).astype(BF16)
        gpy[0, at, HID:] = (grad * silu[at, :]).astype(BF16)

    def back_tokens(first, count):
        at = pl.ds(first, count)

        @pl.loop(0, 4)
        def _(i):
            part_i[i, at, :] = (
                dot_nt(gpy[0, at, 0:HID], wg[i]) + dot_nt(gpy[0, at, HID:], wu[i])
            ).astype(BF16)

    ORDER = (2, 1, 3, 0)

    def down_grads(k):
        i = block(ORDER[k])

        @pl.loop(0, 4)
        def _(f):
            at = pl.ds(pl.multiple_of(f * 256, 256), 256)
            g_dn[k, :, at] = dot_tn(hid[0], rows_c[i, :, at]).astype(BF16)

    def gate_up_grads(k, last=False):
        rows = rows_t.at[block(0)] if k == 0 else rows_y.at[k - 1]

        @pl.loop(0, 4)
        def _(f):
            at = pl.ds(pl.multiple_of(f * 256, 256), 256)
            term = dot_tn(rows[:, at], gpy[k])
            if k == 0:
                acc[at, :] = term
            elif not last:
                acc[at, :] += term
            else:
                both = (acc[at, :] + term).astype(BF16)
                out_gate[0, at, :] = both[:, :HID]
                out_up[0, at, :] = both[:, HID:]

    def rs_copies(m):
        a, b = pl.ds(m * CROWS, QROWS), pl.ds(m * CROWS + QROWS, QROWS)
        s, r = rs_ssem, rs_rsem
        return (
            remote(part_i.at[2, a], x_one.at[m, 0], s.at[m, 0], r.at[m, 0], x_next),
            remote(part_i.at[2, b], x_one.at[m, 1], s.at[m, 1], r.at[m, 1], x_prev),
            remote(part_i.at[1, b], x_left.at[b], s.at[m, 2], r.at[m, 2], x_next),
            remote(part_i.at[3, a], x_right.at[a], s.at[m, 3], r.at[m, 3], x_prev),
            remote(part_i.at[1, a], x_left.at[a], s.at[m, 4], r.at[m, 4], x_next),
            remote(part_i.at[3, b], x_right.at[b], s.at[m, 5], r.at[m, 5], x_prev),
        )

    def add_into(ref, at, other):
        ref[at] = (ref[at].astype(F32) + other.astype(F32)).astype(BF16)

    def rs_first(m):
        for copy in rs_copies(m)[:4]:
            copy.start()

    def rs_pass_on(m):
        copies = rs_copies(m)
        copies[0].wait_recv()
        add_into(part_i, (1, pl.ds(m * CROWS, QROWS)), x_one[m, 0])
        copies[4].start()
        copies[1].wait_recv()
        add_into(part_i, (3, pl.ds(m * CROWS + QROWS, QROWS)), x_one[m, 1])
        copies[5].start()

    total = (send_t, send_c)

    def zr_copy(k, j):
        at = pl.ds(j * CAP, CAP)
        return remote(
            total[k].at[at], ret.at[k, at], zr_ssem.at[k, j], zr_rsem.at[k, j], from_of(j)
        )

    def zr_start(k, m):
        for j in range(max(m * 4, 1), m * 4 + 4):
            zr_copy(k, j).start()
        if m == 0:
            ret[k, 0:CAP, :] = total[k][0:CAP, :]

    def rs_last(m):
        for copy in rs_copies(m)[2:]:
            copy.wait_recv()
        at = pl.ds(m * CROWS, CROWS)
        total[1][at, :] = (
            part_i[0, at, :].astype(F32) + x_left[at, :].astype(F32) + x_right[at, :].astype(F32)
        ).astype(BF16)
        zr_start(1, m)

    def second_layer(m):
        for copy in hd_copies(m)[2:]:
            copy.wait_recv()
        at = hrows(m)
        out = dot_nn(hid[0, at, :], wd[0])
        for i in range(1, 4):
            out += dot_nn(hid[i, at, :], wdx[i - 1])
        total[0][at, :] = out.astype(BF16)
        zr_start(0, 2 * m + 1)
        zr_start(0, 2 * m)

    def back(k):
        for j in range(1, NE):
            zr_copy(k, j).wait_recv()
        spread = jnp.where(
            lax.broadcasted_iota(jnp.int32, (TOK, ROWS), 1) == slot_col, 1.0, 0.0
        ).astype(BF16)
        return dot_nn(spread, ret[k])

    HH = HID // 2
    dn_a, dn_b = pl.ds(0, HH), pl.ds(HH, HH)

    def y_copies():
        s, r = y_ssem, y_rsem
        return (
            remote(g_dn.at[0, dn_a], y_one.at[0], s.at[0], r.at[0], y_next),
            remote(g_dn.at[0, dn_b], y_one.at[1], s.at[1], r.at[1], y_prev),
            remote(g_dn.at[1, dn_b], y_left.at[dn_b], s.at[2], r.at[2], y_next),
            remote(g_dn.at[2, dn_a], y_right.at[dn_a], s.at[3], r.at[3], y_prev),
            remote(g_dn.at[1, dn_a], y_left.at[dn_a], s.at[4], r.at[4], y_next),
            remote(g_dn.at[2, dn_b], y_right.at[dn_b], s.at[5], r.at[5], y_prev),
        )

    for load in loads_d:
        load.wait()
    for copy in wx_copies():
        copy.start()
    ag_send(0, 0)
    z_start(0, 2)
    make_cotangent()
    ag_send(0, 1)
    z_start(0, 3)
    for copy in wx_copies():
        copy.wait_recv()
    begin(wy_sends())
    ag_forward(0, 0)
    ag_send(0, 2)
    z_start(1, 0)
    z_start(1, 1)
    ag_forward(0, 1)
    ty_first(0)
    ag_send(0, 3)
    z_start(1, 2)
    ag_forward(0, 2)
    ty_first(1)
    z_start(1, 3)
    ag_send(1, 0)
    ag_forward(0, 3)
    for n in range(2):
        wy_recvs()[n].wait_recv()
        wy_sends()[2 + n].start()
    ty_first(2)
    ty_forward(0)
    ag_send(1, 1)
    for load in loads:
        load.wait()
    first_layer(0)
    begin(hd_copies(0))
    ag_send(1, 2)
    ag_forward(1, 0)
    ag_send(1, 3)
    ty_first(3)
    ty_forward(1)
    first_layer(1)
    ag_forward(1, 1)
    ty_forward(2)
    forward(hd_copies(0))
    ag_forward(1, 2)
    ag_wait(1, 0)
    ag_wait(1, 1)
    back_hidden(0, HROWS)
    begin(gp_copies(0))
    for k in range(2):
        for j in range(1, NE):
            z_copy(k, j).wait_send()
    for copy in wy_recvs()[2:]:
        copy.wait_recv()
    second_layer(0)
    back_tokens(0, HROWS)
    ty_forward(3)
    ag_forward(1, 3)
    begin(hd_copies(1))
    rs_first(1)
    ag_wait(1, 2)
    back_hidden(2 * CROWS, CROWS)
    ag_wait(1, 3)
    back_hidden(3 * CROWS, CROWS)
    begin(gp_copies(1))
    ys = y_copies()
    down_grads(0)
    ys[0].start()
    ys[1].start()
    forward(hd_copies(1))
    back_tokens(3 * CROWS, CROWS)
    rs_first(3)
    rs_pass_on(1)
    back_tokens(2 * CROWS, CROWS)
    rs_first(2)
    second_layer(1)
    forward(gp_copies(0))
    down_grads(1)
    ys[2].start()
    down_grads(2)
    ys[3].start()
    rs_pass_on(3)
    rs_first(0)
    rs_pass_on(2)
    rs_last(1)
    gate_up_grads(0)
    forward(gp_copies(1))
    rs_last(3)
    ys[0].wait_recv()
    add_into(g_dn, (1, dn_a), y_one[0])
    ys[4].start()
    ys[1].wait_recv()
    add_into(g_dn, (2, dn_b), y_one[1])
    ys[5].start()
    rs_pass_on(0)
    for m in range(CH):
        ty_copies(m)[2].wait_recv()
        ty_copies(m)[3].wait_recv()
    gate_up_grads(3)
    rs_last(2)
    gate_up_grads(1)
    rs_last(0)
    down_grads(3)
    mixed[...] = (weight * back(0).astype(BF16).astype(F32)).astype(BF16)
    for m in range(CH):
        ty_copies(m)[4].wait_recv()
        ty_copies(m)[5].wait_recv()
    for m in range(2):
        gp_copies(m)[2].wait_recv()
        gp_copies(m)[3].wait_recv()
    gate_up_grads(2, last=True)
    for copy in ys[2:]:
        copy.wait_recv()
    out_down[0] = (
        g_dn[3].astype(F32) + y_left[...].astype(F32) + y_right[...].astype(F32)
    ).astype(BF16)
    grad_tokens[...] = back(1).astype(BF16)

    for k in range(2):
        for c in range(CH):
            for copy in ag_copies(k, c):
                copy.wait_send()
        for copy in hd_copies(k) + gp_copies(k):
            copy.wait_send()
        for j in range(1, NE):
            zr_copy(k, j).wait_send()
    for m in range(CH):
        for copy in ty_copies(m) + rs_copies(m):
            copy.wait_send()
    for copy in wx_copies() + list(wy_sends()) + list(ys):
        copy.wait_send()


def finish_kernel(*refs):
    n = len(refs) // 2
    sem = refs[-1]
    copies = [pltpu.make_async_copy(refs[i], refs[n + i], sem.at[i]) for i in range(n)]
    for copy in copies:
        copy.start()
    for copy in copies:
        copy.wait()


def finish(*parts):
    far = pl.BlockSpec(memory_space=pl.ANY)
    return pl.pallas_call(
        finish_kernel,
        out_shape=tuple(jax.ShapeDtypeStruct(p.shape, p.dtype) for p in parts),
        in_specs=[pl.BlockSpec(memory_space=pltpu.VMEM)] * len(parts),
        out_specs=(far,) * len(parts),
        scratch_shapes=[pltpu.SemaphoreType.DMA((len(parts),))],
        compiler_params=pltpu.CompilerParams(vmem_limit_bytes=2**20),
        name="hand_over",
    )(*parts)


def body(tokens, expert_id, route_weight, cluster_id, out_grad, w_gate, w_up, w_down):
    vmem, far = pl.BlockSpec(memory_space=pltpu.VMEM), pl.BlockSpec(memory_space=pl.ANY)
    dma = pltpu.SemaphoreType.DMA
    rollouts = cluster_id.shape[0]
    parts = pl.pallas_call(
        kernel,
        out_shape=(
            pltpu.VMEM((TOK, FB), BF16),
            pltpu.VMEM((TOK, FB), BF16),
            pltpu.VMEM((1, FB, HID), BF16),
            pltpu.VMEM((1, FB, HID), BF16),
            pltpu.VMEM((1, HID, FB), BF16),
        ),
        in_specs=[vmem] * 3 + [far] * 5,
        out_specs=(vmem,) * 5,
        scratch_shapes=[
            pltpu.VMEM((TOK, FB), BF16),
            pltpu.VMEM((TOK, FB), BF16),
            pltpu.VMEM((ROWS, FB), BF16),
            pltpu.VMEM((ROWS, FB), BF16),
            pltpu.VMEM((4, ROWS, FB), BF16),
            pltpu.VMEM((4, ROWS, FB), BF16),
            pltpu.VMEM((4, FB, HID), BF16),
            pltpu.VMEM((4, FB, HID), BF16),
            pltpu.VMEM((4, HID, FB), BF16),
            pltpu.VMEM((3, HID, FB), BF16),
            pltpu.VMEM((ROWS, HID), F32),
            pltpu.VMEM((ROWS, HID), F32),
            pltpu.VMEM((4, ROWS, HID), BF16),
            pltpu.VMEM((4, ROWS, 2 * HID), BF16),
            pltpu.VMEM((3, ROWS, FB), BF16),
            pltpu.VMEM((CH, 2, QROWS, FB), BF16),
            pltpu.VMEM((FB, 2 * HID), F32),
            pltpu.VMEM((4, ROWS, FB), BF16),
            pltpu.VMEM((CH, 2, QROWS, FB), BF16),
            pltpu.VMEM((ROWS, FB), BF16),
            pltpu.VMEM((ROWS, FB), BF16),
            pltpu.VMEM((2, ROWS, FB), BF16),
            pltpu.VMEM((4, HID, FB), BF16),
            pltpu.VMEM((2, HID // 2, FB), BF16),
            pltpu.VMEM((HID, FB), BF16),
            pltpu.VMEM((HID, FB), BF16),
            dma((14,)),
            dma((2, NE)),
            dma((2, NE)),
            dma((2, CH, 4)),
            dma((2, CH, 4)),
            dma((CH, 6)),
            dma((CH, 6)),
            dma((2, NE)),
            dma((2, NE)),
            dma((3,)),
            dma((3,)),
            dma((4,)),
            dma((4,)),
            dma((CH, 6)),
            dma((CH, 6)),
            dma((2, 4)),
            dma((2, 4)),
            dma((2, 4)),
            dma((2, 4)),
            dma((6,)),
            dma((6,)),
        ],
        compiler_params=pltpu.CompilerParams(
            collective_id=0, has_side_effects=True, vmem_limit_bytes=LIMIT * 2**20
        ),
        name="expert_layer",
    )(
        expert_id.reshape(1, TOK),
        route_weight.reshape(1, TOK),
        cluster_id.reshape(1, rollouts),
        tokens,
        out_grad,
        w_gate,
        w_up,
        w_down,
    )
    return finish(*parts)


def solution(mesh):
    placed = (
        P(("rep", "exp"), "tp"),
        P(("rep", "exp"), None),
        P(("rep", "exp"), None),
        P(),
        P(("rep", "exp"), "tp"),
        P("exp", None, "tp"),
        P("exp", None, "tp"),
        P("exp", "tp", None),
    )
    return jax.shard_map(
        body,
        mesh=mesh,
        in_specs=placed,
        out_specs=(
            P(("rep", "exp"), "tp"),
            P(("rep", "exp"), "tp"),
            P("exp", "rep", "tp"),
            P("exp", "rep", "tp"),
            P("exp", "tp", "rep"),
        ),
        check_vma=False,
    )
```
